32 devices in a mesh: chan: 4 (over z), tm: 8 (over y, x, core).
Axes of the slice: x: 2, y: 2, z: 4, core: 2. Of those that a mesh axis runs over, the one named last changes fastest.
Arguments:
- symbols: int32 [32, 65536], P('chan', 'tm'), may hold values from 0 to 63
- incidence: int32 [128, 6], P('chan'), may hold values from 0 to 31, as said below
- delays: int32 [128, 6], P('chan'), may hold values from 0 to 63
- gains: float32 [2, 128, 6], P(None, 'chan'), may hold values from -4 to 4
- echoes: bfloat16 [2, 128, 65536], P(None, 'chan', 'tm'), may hold values from -6 to 6
Outputs:
- cancelled: bfloat16 [2, 128, 65536], P(None, 'chan', 'tm')
- weights: float32 [2, 128, 384], P(None, 'chan')
The draws below stay inside these ranges and needn't reach their ends.
Inputs may be any that keep to these rules, and one draw needn't show every extreme that they name: `incidence`: row r names 6 distinct illuminators, all owned by chan index c = r // 32 or the next index c + 1 taken cyclically: ids from c * 8 to (c + 2) * 8 - 1, modulo 32.
All inputs are finite; a program needn't handle non-finite values.
Results may differ from the reference program's by a relative error of at most 0.024.
Values may be sent and summed in bfloat16 or wider, within the bound.
A program may use at most 128 MiB of HBM per device.

```python
import math
import jax
import jax.numpy as jnp
from jax import lax

FOURIER_LENGTH = 8192
ACTIVE = 6817
DELAYS = 64
PER_RECV = 6
I_DEV = 8
R_DEV = 32
ILLUM = 32
RECV = 128
SAMPLES = 65536


def draw_incidence(key, part):
    owner_base = jnp.arange(RECV, dtype=jnp.int32) // R_DEV
    row_keys = jax.random.split(jax.random.fold_in(key, 11), RECV)
    chosen_slots = jax.vmap(lambda row_key: jax.random.permutation(row_key, 2 * I_DEV)[:PER_RECV])(row_keys).astype(jnp.int32)
    owner_chan = (owner_base[:, None] + chosen_slots // I_DEV) % (ILLUM // I_DEV)
    return (owner_chan * I_DEV + chosen_slots % I_DEV).astype(jnp.int32)


def touch_ends(entries, key, smallest, high):
    longest = entries.shape.index(max(entries.shape))
    spots = []
    for shift in (0, 1):
        where = [jax.random.randint(jax.random.fold_in(key, axis), (), 0, length) for axis, length in enumerate(entries.shape)]
        where[longest] = (where[longest] + shift) % entries.shape[longest]
        spots.append(tuple(where))
    return entries.at[spots[0]].set(smallest).at[spots[1]].set(high)


def levels(stream_key, dims, cuts, smallest, top_value):
    level = 1.0
    for position, parts in cuts:
        draws = jax.random.uniform(jax.random.fold_in(jax.random.fold_in(stream_key, 6), position), (parts,), jnp.float32, smallest / len(cuts), top_value / len(cuts))
        level = level * jnp.repeat(jnp.exp(draws), dims[position] // parts).reshape((-1,) + (1,) * (len(dims) - 1 - position))
    return level


def normal_values(stream_key, extent, scale, reach, cuts=(), kind=jnp.bfloat16):
    values = jax.random.normal(stream_key, extent, jnp.float32) * scale
    if len(cuts) > 0:
        values = levels(stream_key, extent, cuts, -0.22, 0.18) * values
    return jnp.clip(values, min=-reach, max=reach).astype(kind)


def setup_inputs(seed: int = 0) -> dict:
    streams_of = jax.random.split(jax.random.key(seed), 6)
    symbols = touch_ends(jax.random.randint(streams_of[0], (ILLUM, SAMPLES), 0, 64), jax.random.fold_in(streams_of[0], 1), 0, 63).astype(jnp.int32)
    incidence = draw_incidence(jax.random.fold_in(streams_of[5], 71), 0)
    delays = touch_ends(jax.random.randint(streams_of[2], (RECV, PER_RECV), 0, DELAYS), jax.random.fold_in(streams_of[2], 1), 0, DELAYS - 1).astype(jnp.int32)
    gains = normal_values(streams_of[3], (2, RECV, PER_RECV), 1.0, 4.0, ((1, 4),), jnp.float32)
    echoes = normal_values(streams_of[4], (2, RECV, SAMPLES), 1.0, 6.0, ((1, 4), (2, 8)))
    return {"symbols": symbols, "incidence": incidence, "delays": delays, "gains": gains, "echoes": echoes}


loading = 0.1

def reference(symbols, incidence, delays, gains, echoes):
    emitter_number = symbols.shape[0]
    samples = symbols.shape[1]
    processor_portions = samples // FOURIER_LENGTH
    blocks = samples // DELAYS
    key_len = PER_RECV * DELAYS
    inphase_amplitude = (2 * (symbols % 8) - 7).astype(jnp.float32) / math.sqrt(42.0)
    quadrature_amplitude = (2 * (symbols // 8) - 7).astype(jnp.float32) / math.sqrt(42.0)
    subcarrier = jnp.arange(FOURIER_LENGTH, dtype=jnp.int32) - FOURIER_LENGTH // 2
    occupied_tones = (jnp.abs(subcarrier) <= (ACTIVE - 1) // 2).astype(jnp.float32)
    tone_symbols = (inphase_amplitude + 1j * quadrature_amplitude).reshape(emitter_number, processor_portions, FOURIER_LENGTH) * occupied_tones
    waveform_samples = jnp.fft.ifft(tone_symbols, axis=-1) * FOURIER_LENGTH
    alternate = (1 - 2 * (jnp.arange(FOURIER_LENGTH, dtype=jnp.int32) % 2)).astype(jnp.float32) / math.sqrt(ACTIVE)
    waveform_samples = (waveform_samples * alternate).reshape(emitter_number, samples)
    ref_re = jnp.real(waveform_samples).astype(jnp.bfloat16)
    ref_im = jnp.imag(waveform_samples).astype(jnp.bfloat16)
    padded = jnp.pad(jnp.stack([ref_re, ref_im], axis=1), ((0, 0), (0, 0), (DELAYS, 0)))
    pieces = padded.astype(jnp.float32).reshape(emitter_number, 2, blocks + 1, DELAYS)
    frames = jnp.concatenate([pieces[:, :, :-1], pieces[:, :, 1:]], axis=3)
    frame_freq = jnp.fft.fft(frames[:, 0] + 1j * frames[:, 1], axis=-1)
    current = pieces[:, 0, 1:] + 1j * pieces[:, 1, 1:]
    current = jnp.pad(current, ((0, 0), (0, 0), (0, DELAYS)))
    current_freq = jnp.fft.fft(current, axis=-1)
    pair_freq = jnp.einsum('iqf,jqf->fij', jnp.conj(frame_freq), current_freq)
    lag_index = DELAYS - jnp.arange(DELAYS, dtype=jnp.int32)
    corr = (jnp.fft.fft(pair_freq, axis=0) / (2 * DELAYS))[lag_index] / samples
    corr_re = jnp.transpose(jnp.real(corr), (1, 2, 0))
    corr_im = jnp.transpose(jnp.imag(corr), (1, 2, 0))
    lag_diff = jnp.arange(DELAYS, dtype=jnp.int32)[:, None] - jnp.arange(DELAYS, dtype=jnp.int32)[None, :]
    below_diag = lag_diff >= 0
    forward_lag = jnp.clip(lag_diff, 0, DELAYS - 1)
    backward_lag = jnp.clip(-lag_diff, 0, DELAYS - 1)
    identity = jnp.eye(key_len, dtype=jnp.float32)

    def per_receiver(inputs):
        chosen, lag_values, gain, echo = inputs
        rows = padded[chosen]
        shifted = jax.vmap(lambda ref_row, lag_value: lax.dynamic_slice_in_dim(ref_row, DELAYS - lag_value, samples, 1))(rows, lag_values).astype(jnp.float32)
        direct_re = lax.optimization_barrier(jnp.sum(gain[0][:, None] * shifted[:, 0] - gain[1][:, None] * shifted[:, 1], axis=0))
        direct_im = lax.optimization_barrier(jnp.sum(gain[0][:, None] * shifted[:, 1] + gain[1][:, None] * shifted[:, 0], axis=0))
        received = jnp.stack([echo[0].astype(jnp.float32) + direct_re, echo[1].astype(jnp.float32) + direct_im]).astype(jnp.bfloat16)
        signal = received.astype(jnp.float32).reshape(2, blocks, DELAYS)
        signal_c = jnp.pad(signal[0] + 1j * signal[1], ((0, 0), (0, DELAYS)))
        signal_freq = jnp.fft.fft(signal_c, axis=-1)
        chosen_freq = frame_freq[chosen]
        cross_freq = jnp.einsum('kqf,qf->fk', jnp.conj(chosen_freq), signal_freq)
        cross = (jnp.fft.fft(cross_freq, axis=0) / (2 * DELAYS))[lag_index] / samples
        cross_re = jnp.real(cross).T.reshape(key_len)
        cross_im = jnp.imag(cross).T.reshape(key_len)
        sub_re = corr_re[chosen][:, chosen]
        sub_im = corr_im[chosen][:, chosen]
        swap_re = jnp.transpose(sub_re, (1, 0, 2))
        swap_im = jnp.transpose(sub_im, (1, 0, 2))
        gram_re = jnp.where(below_diag, sub_re[:, :, forward_lag], swap_re[:, :, backward_lag])
        gram_im = jnp.where(below_diag, sub_im[:, :, forward_lag], -swap_im[:, :, backward_lag])
        gram_re = jnp.transpose(gram_re, (0, 2, 1, 3)).reshape(key_len, key_len) + loading * identity
        gram_im = jnp.transpose(gram_im, (0, 2, 1, 3)).reshape(key_len, key_len)
        system = jnp.concatenate([jnp.concatenate([gram_re, -gram_im], axis=1), jnp.concatenate([gram_im, gram_re], axis=1)], axis=0)
        factor = jnp.linalg.cholesky(system)
        solved = jax.scipy.linalg.cho_solve((factor, True), jnp.concatenate([cross_re, cross_im]))
        rounded = lax.optimization_barrier(solved.astype(jnp.bfloat16)).astype(jnp.float32)
        tap_c = rounded[:key_len].reshape(PER_RECV, DELAYS) + 1j * rounded[key_len:].reshape(PER_RECV, DELAYS)
        tap_freq = jnp.fft.fft(jnp.pad(tap_c, ((0, 0), (0, DELAYS))), axis=-1)
        proj_freq = jnp.einsum('kqf,kf->qf', chosen_freq, tap_freq)
        projected = jnp.fft.ifft(proj_freq, axis=-1)[:, DELAYS:]
        result = jnp.stack([signal[0].reshape(samples) - jnp.real(projected).reshape(samples), signal[1].reshape(samples) - jnp.imag(projected).reshape(samples)]).astype(jnp.bfloat16)
        return (result, jnp.stack([solved[:key_len], solved[key_len:]]))
    cancelled, weights = lax.map(per_receiver, (incidence, delays, jnp.transpose(gains, (1, 0, 2)), jnp.transpose(echoes, (1, 0, 2))))
    return (jnp.transpose(cancelled, (1, 0, 2)), jnp.transpose(weights, (1, 0, 2)))
```

```python
import math

import jax
import jax.numpy as jnp
from jax import lax
from jax.experimental import pallas as pl
from jax.experimental.pallas import tpu as pltpu
from jax.sharding import PartitionSpec as P

ACTIVE = 6817
DELAYS = 64
PER_RECV = 6


loading = 0.1
LANES = 128
MIB = 2**20
HIGHEST = lax.Precision.HIGHEST


def passed_along(array, axis, by):
    peers = lax.axis_size(axis)
    return lax.ppermute(array, axis, [(i, (i + by) % peers) for i in range(peers)])


def from_behind(block, axis, distance):
    devices = range(lax.axis_size(axis))
    route = [(i - distance, i) for i in devices if i - distance in devices]
    return lax.ppermute(block, axis, route)


def rotation_angle_grid(row_count, col_count, period):
    product = (
        jnp.arange(row_count, dtype=jnp.int32)[:, None]
        * jnp.arange(col_count, dtype=jnp.int32)[None, :]
    )
    phases = (product % period).astype(jnp.float32) * (2.0 * math.pi / period)
    return (jnp.cos(phases), jnp.sin(phases))


def complex_multiply_result(pattern, left_pair, right_pair):
    real_part = jnp.einsum(pattern, left_pair[0], right_pair[0], precision=HIGHEST) - jnp.einsum(
        pattern, left_pair[1], right_pair[1], precision=HIGHEST
    )
    imag_part = jnp.einsum(pattern, left_pair[0], right_pair[1], precision=HIGHEST) + jnp.einsum(
        pattern, left_pair[1], right_pair[0], precision=HIGHEST
    )
    return (real_part, imag_part)


def remodulate(symbols):
    emitter_number, length = symbols.shape
    column_entries = 128
    increment_spacing = length // column_entries
    inphase_amplitude = (2 * (symbols % 8) - 7).astype(jnp.float32) / math.sqrt(42.0)
    quadrature_amplitude = (2 * (symbols // 8) - 7).astype(jnp.float32) / math.sqrt(42.0)
    subcarrier = jnp.arange(length, dtype=jnp.int32) - length // 2
    occupied_tones = (jnp.abs(subcarrier) <= (ACTIVE - 1) // 2).astype(jnp.float32)
    tone_symbols = (
        (inphase_amplitude * occupied_tones).reshape(
            emitter_number, increment_spacing, column_entries
        ),
        (quadrature_amplitude * occupied_tones).reshape(
            emitter_number, increment_spacing, column_entries
        ),
    )
    partial_result = complex_multiply_result(
        "mb,nbd->nmd",
        rotation_angle_grid(increment_spacing, increment_spacing, increment_spacing),
        tone_symbols,
    )
    twiddle = rotation_angle_grid(increment_spacing, column_entries, length)
    partial_result = (
        partial_result[0] * twiddle[0] - partial_result[1] * twiddle[1],
        partial_result[0] * twiddle[1] + partial_result[1] * twiddle[0],
    )
    frequency_spectrum = complex_multiply_result(
        "pho,oj->phj",
        partial_result,
        rotation_angle_grid(column_entries, column_entries, column_entries),
    )
    alternate = (1 - 2 * (jnp.arange(length, dtype=jnp.int32) % 2)).astype(jnp.float32) / math.sqrt(
        ACTIVE
    )
    real_part = (
        jnp.swapaxes(frequency_spectrum[0], 1, 2).reshape(emitter_number, length) * alternate
    )
    imag_part = (
        jnp.swapaxes(frequency_spectrum[1], 1, 2).reshape(emitter_number, length) * alternate
    )
    return jnp.stack([real_part, imag_part], axis=1).astype(jnp.bfloat16)


def lanes_of(shape):
    return lax.broadcasted_iota(jnp.int32, shape, len(shape) - 1)


def rows_of(shape):
    return lax.broadcasted_iota(jnp.int32, shape, len(shape) - 2)


def half_turn(block):
    return pltpu.roll(block, LANES // 2, 1)


def signal_matrix(re, im):
    low = lanes_of(re.shape) < LANES // 2
    turned_re, turned_im = half_turn(re), half_turn(im)
    return jnp.concatenate(
        [
            jnp.where(low, re, turned_im),
            jnp.where(low, turned_re, im),
            jnp.where(low, im, -turned_re),
            jnp.where(low, turned_im, -re),
        ],
        axis=0,
    ).astype(jnp.bfloat16)


def fold_lags(product):
    half = LANES // 2
    shape = (half, LANES)
    earlier = lanes_of(shape) % half < rows_of(shape)
    total = jnp.where(earlier, half_turn(product[:half]), product[half:])
    rows = half // 2
    while rows >= 8:
        total = total[:rows] + pltpu.roll(total[rows:], LANES - rows, 1)
        rows //= 2
    for step in (4, 2, 1):
        total = total + pltpu.roll(pltpu.roll(total, LANES - step, 1), 8 - step, 0)
    return total[:1]


def front_kernel(
    slots, delays, gains, x_ref, xp_ref, echo_ref, recv_ref, corr_ref, cross_ref, fq_ref, ft_ref
):
    window, _, rows, _ = x_ref.shape
    recv_count = echo_ref.shape[1]
    lane = lanes_of((rows, LANES))
    low = lane < LANES // 2

    def frame(i, carry):
        parts = []
        for c in range(2):
            x = x_ref[i, c]
            parts += [half_turn(jnp.where(low, x, xp_ref[i, c])), x]
        whole = jnp.concatenate(parts, axis=0)
        fq_ref[i] = whole.astype(jnp.bfloat16)
        ft_ref[i] = whole.T.astype(jnp.bfloat16)
        return carry

    lax.fori_loop(0, window, frame, 0)

    def pairs(j, carry):
        matrix = signal_matrix(x_ref[j, 0], x_ref[j, 1])
        for i in range(window):
            product = jnp.dot(ft_ref[i], matrix, preferred_element_type=jnp.float32)
            corr_ref[j, i : i + 1, :] = fold_lags(product)
        return carry

    lax.fori_loop(0, window, pairs, 0)

    def receiver(r, carry):
        re = jnp.zeros((rows, LANES), jnp.float32)
        im = jnp.zeros((rows, LANES), jnp.float32)
        for k in range(PER_RECV):
            s = slots[r, k]
            d = delays[r, k]
            g_re = gains[0, r, k]
            g_im = gains[1, r, k]
            wrapped = lane >= LANES - d
            y_re = pltpu.roll(jnp.where(wrapped, xp_ref[s, 0], x_ref[s, 0]), d, 1)
            y_im = pltpu.roll(jnp.where(wrapped, xp_ref[s, 1], x_ref[s, 1]), d, 1)
            re = re + (g_re * y_re - g_im * y_im)
            im = im + (g_re * y_im + g_im * y_re)
        re = (echo_ref[0, r].astype(jnp.float32) + re).astype(jnp.bfloat16)
        im = (echo_ref[1, r].astype(jnp.float32) + im).astype(jnp.bfloat16)
        recv_ref[0, r] = re
        recv_ref[1, r] = im
        matrix = signal_matrix(re.astype(jnp.float32), im.astype(jnp.float32))
        for k in range(PER_RECV):
            product = jnp.dot(ft_ref[slots[r, k]], matrix, preferred_element_type=jnp.float32)
            cross_ref[r, k : k + 1, :] = fold_lags(product)
        return carry

    lax.fori_loop(0, recv_count, receiver, 0)


def back_kernel(slots, taps_ref, fq_ref, recv_ref, out_ref):
    recv_count, rows = recv_ref.shape[1:3]
    half = LANES // 2
    shape = (LANES, LANES)
    place = lanes_of(shape) % half
    row = rows_of(shape)
    valid = ((row < half) & (place < row)) | ((row >= half) & (place >= row - half))
    low = lanes_of((LANES, LANES)) < half
    low_half = lanes_of((rows, LANES)) < half

    def receiver(r, carry):
        total = jnp.zeros((4 * rows, LANES), jnp.float32)
        for k in range(PER_RECV):
            base = jnp.broadcast_to(taps_ref[r, k : k + 1, :], shape)
            band = pltpu.roll(base, half, 1, stride=1, stride_axis=0)
            band = jnp.where(valid, band, 0.0).astype(jnp.bfloat16)
            total = total + jnp.dot(
                fq_ref[slots[r, k]], band, preferred_element_type=jnp.float32
            )
        turned = half_turn(total[2 * rows :])
        both = total[: 2 * rows] + jnp.where(low, -turned, turned)
        first, second = both[:rows], both[rows:]
        re = jnp.where(low_half, first, half_turn(second))
        im = jnp.where(low_half, half_turn(first), second)
        out_ref[0, r] = (recv_ref[0, r].astype(jnp.float32) - re).astype(jnp.bfloat16)
        out_ref[1, r] = (recv_ref[1, r].astype(jnp.float32) - im).astype(jnp.bfloat16)
        return carry

    lax.fori_loop(0, recv_count, receiver, 0)


def times_i(block):
    pieces = []
    for start in range(0, block.shape[1], LANES):
        turned = half_turn(block[:, start : start + LANES])
        pieces.append(jnp.where(lanes_of(turned.shape) < LANES // 2, -turned, turned))
    return jnp.concatenate(pieces, axis=1)


def complex_dot(left, right):
    return jnp.dot(left, right, precision=HIGHEST, preferred_element_type=jnp.float32)


def as_real(block):
    return jnp.concatenate([block, times_i(block)], axis=0)


def invert(blocks):
    size = blocks[0].shape[0]
    lane = lanes_of(blocks[0].shape)
    row_id = rows_of(blocks[0].shape)
    lane_row = lanes_of((1, LANES))
    blocks = list(blocks)
    for j in range(size):
        for s, a in enumerate(blocks):
            pivot = 1.0 / a[j : j + 1, j : j + 1]
            row = jnp.where(lane_row == j, 1.0, jnp.where(lane_row == size + j, 0.0, a[j : j + 1]))
            row = row * pivot
            turned = half_turn(row)
            row_i = jnp.where(lane_row < size, -turned, turned)
            rest = jnp.where((lane == j) | (lane == size + j), 0.0, a)
            rest = rest - a[:, j : j + 1] * row - a[:, size + j : size + j + 1] * row_i
            blocks[s] = jnp.where(row_id == j, row, rest)
    return blocks


def solve_kernel(slots, vr_ref, vi_ref, rhs_ref, out_ref, a_ref, d_ref):
    share = rhs_ref.shape[0]
    size = DELAYS
    window = math.isqrt(vr_ref.shape[0])
    shape = (size, LANES)
    lane, row_id = lanes_of(shape), rows_of(shape)
    low = lane < size
    unit = jnp.where(lane == row_id, jnp.float32(loading), 0.0)
    end = PER_RECV * LANES

    def build(index, carry):
        s, k = index // PER_RECV, index % PER_RECV
        start = pl.multiple_of(k * size, size)
        first = slots[s, k]
        for l in range(PER_RECV):
            at = first * window + slots[s, l]
            re = jnp.broadcast_to(vr_ref[at], shape)
            im = jnp.broadcast_to(vi_ref[at], shape)
            block = jnp.where(
                low,
                pltpu.roll(re, 0, 1, stride=1, stride_axis=0),
                pltpu.roll(im, size, 1, stride=1, stride_axis=0),
            )
            block = block + jnp.where(k == l, unit, 0.0)
            a_ref[s, pl.ds(start, size), l * LANES : (l + 1) * LANES] = block
        side = rhs_ref[s, pl.ds(start, size), :]
        a_ref[s, pl.ds(start, size), end : end + LANES] = jnp.where(
            lane == 0, side[:, 0:1], jnp.where(lane == size, side[:, 1:2], 0.0)
        )
        return carry

    lax.fori_loop(0, share * PER_RECV, build, 0)

    def eliminate(p, carry):
        at_row = pl.multiple_of(p * size, size)
        at_col = pl.multiple_of(p * LANES, LANES)
        blocks = [a_ref[s, pl.ds(at_row, size), pl.ds(at_col, LANES)] for s in range(share)]
        for s, block in enumerate(invert(blocks)):
            d_ref[s] = block
        for step in range(PER_RECV):

            @pl.when(p == step)
            def _():
                top, left = step * size, (step + 1) * LANES
                for s in range(share):
                    right = a_ref[s, top : top + size, left:]
                    scaled = complex_dot(d_ref[s], as_real(right))
                    a_ref[s, top : top + size, left:] = scaled
                    if step < PER_RECV - 1:
                        below = a_ref[s, top + size :, left - LANES : left]
                        a_ref[s, top + size :, left:] -= complex_dot(below, as_real(scaled))

        return carry

    lax.fori_loop(0, PER_RECV, eliminate, 0)
    for s in range(share):
        known = None
        for p in reversed(range(PER_RECV)):
            top, left = p * size, (p + 1) * LANES
            found = a_ref[s, top : top + size, end : end + LANES]
            if known is not None:
                found = found - complex_dot(a_ref[s, top : top + size, left:end], known)
            out_ref[s, top : top + size, :] = found
            found = as_real(found)
            known = found if known is None else jnp.concatenate([found, known], axis=0)


def kernel_call(body, outs, scalars, arrays, scratch=()):
    spec_smem = pl.BlockSpec(memory_space=pltpu.SMEM)
    spec_vmem = pl.BlockSpec(memory_space=pltpu.VMEM)
    return pl.pallas_call(
        body,
        out_shape=outs,
        in_specs=[spec_smem] * len(scalars) + [spec_vmem] * len(arrays),
        out_specs=jax.tree.map(lambda _: spec_vmem, outs),
        scratch_shapes=list(scratch),
        compiler_params=pltpu.CompilerParams(vmem_limit_bytes=48 * MIB),
    )(*scalars, *arrays)


def local(symbols, incidence, delays, gains, echoes):
    local_refs = remodulate(symbols)
    owned = local_refs.shape[0]
    length = local_refs.shape[2]
    rows = length // LANES
    taps_count = PER_RECV * DELAYS
    chan_count = lax.axis_size("chan")
    chan_index = lax.axis_index("chan")
    tm_count = lax.axis_size("tm")
    tm_index = lax.axis_index("tm")
    window_count = 2 * owned
    recv_count = echoes.shape[1]
    following = passed_along(local_refs, "chan", -1)
    window = jnp.concatenate([local_refs, following], axis=0)
    previous = from_behind(window[:, :, length - DELAYS :], "tm", 1)
    previous = jnp.pad(previous, ((0, 0), (0, 0), (LANES - DELAYS, 0)))[:, :, None, :]
    x = window.reshape(window_count, 2, rows, LANES)
    xp = jnp.concatenate([previous, x[:, :, :-1]], axis=2).astype(jnp.float32)
    x = x.astype(jnp.float32)
    owner_chan = incidence // owned
    slot = (owner_chan - chan_index) % chan_count * owned + incidence % owned
    received, corr_part, cross_part, frames = kernel_call(
        front_kernel,
        (
            jax.ShapeDtypeStruct((2, recv_count, rows, LANES), jnp.bfloat16),
            jax.ShapeDtypeStruct((window_count, window_count, LANES), jnp.float32),
            jax.ShapeDtypeStruct((recv_count, PER_RECV, LANES), jnp.float32),
            jax.ShapeDtypeStruct((window_count, 4 * rows, LANES), jnp.bfloat16),
        ),
        (slot, delays, gains),
        (x, xp, echoes.reshape(2, recv_count, rows, LANES)),
        (pltpu.VMEM((window_count, LANES, 4 * rows), jnp.bfloat16),),
    )
    share = recv_count // tm_count
    scale = 1.0 / (length * tm_count)
    corr, cross_whole = lax.psum((corr_part, cross_part), "tm")
    corr = corr * scale
    cross = lax.dynamic_slice_in_dim(cross_whole, tm_index * share, share, 0) * scale
    mine = lax.dynamic_slice_in_dim(slot, tm_index * share, share, 0)
    swapped = jnp.swapaxes(corr, 0, 1)
    gap = jnp.zeros(corr.shape[:2] + (1,), jnp.float32)

    def diagonals(ahead, behind, sign):
        line = jnp.concatenate(
            [ahead[..., :1], sign * behind[..., 1:], gap, jnp.flip(ahead[..., 1:], axis=-1)], axis=-1
        )
        return line.reshape(window_count * window_count, 1, LANES)

    vr = diagonals(swapped[..., :DELAYS], corr[..., :DELAYS], 1.0)
    vi = diagonals(swapped[..., DELAYS:], corr[..., DELAYS:], -1.0)
    rhs = cross.reshape(share, PER_RECV, 2, DELAYS).swapaxes(2, 3).reshape(share, taps_count, 2)
    solved = kernel_call(
        solve_kernel,
        jax.ShapeDtypeStruct((share, taps_count, LANES), jnp.float32),
        (mine,),
        (vr, vi, rhs),
        (
            pltpu.VMEM((share, taps_count, (PER_RECV + 1) * LANES), jnp.float32),
            pltpu.VMEM((share, DELAYS, LANES), jnp.float32),
        ),
    )
    local_weights = jnp.stack([solved[:, :, 0], solved[:, :, DELAYS]])
    weights = lax.all_gather(local_weights, "tm", axis=1, tiled=True)
    taps = weights.astype(jnp.bfloat16).astype(jnp.float32)
    taps = taps.reshape(2, recv_count, PER_RECV, DELAYS).transpose(1, 2, 0, 3)
    taps = taps.reshape(recv_count, PER_RECV, LANES)
    cancelled = kernel_call(
        back_kernel,
        jax.ShapeDtypeStruct((2, recv_count, rows, LANES), jnp.bfloat16),
        (slot,),
        (taps, frames, received),
    )
    return (cancelled.reshape(2, recv_count, length), weights)


def solution(mesh):
    in_specs = (
        P("chan", "tm"),
        P("chan", None),
        P("chan", None),
        P(None, "chan", None),
        P(None, "chan", "tm"),
    )
    out_specs = (P(None, "chan", "tm"), P(None, "chan", None))
    return jax.shard_map(local, mesh=mesh, in_specs=in_specs, out_specs=out_specs, check_vma=False)
```

```python
import math

import jax
import jax.numpy as jnp
from jax import lax
from jax.experimental import pallas as pl
from jax.experimental.pallas import tpu as pltpu
from jax.sharding import PartitionSpec as P

ACTIVE = 6817
DELAYS = 64
PER_RECV = 6


loading = 0.1
LANES = 128
MIB = 2**20
HIGHEST = lax.Precision.HIGHEST


def passed_along(array, axis, by):
    peers = lax.axis_size(axis)
    return lax.ppermute(array, axis, [(i, (i + by) % peers) for i in range(peers)])


def from_behind(block, axis, distance):
    devices = range(lax.axis_size(axis))
    route = [(i - distance, i) for i in devices if i - distance in devices]
    return lax.ppermute(block, axis, route)


def rotation_angle_grid(row_count, col_count, period):
    product = (
        jnp.arange(row_count, dtype=jnp.int32)[:, None]
        * jnp.arange(col_count, dtype=jnp.int32)[None, :]
    )
    phases = (product % period).astype(jnp.float32) * (2.0 * math.pi / period)
    return (jnp.cos(phases), jnp.sin(phases))


def complex_multiply_result(pattern, left_pair, right_pair):
    real_part = jnp.einsum(pattern, left_pair[0], right_pair[0], precision=HIGHEST) - jnp.einsum(
        pattern, left_pair[1], right_pair[1], precision=HIGHEST
    )
    imag_part = jnp.einsum(pattern, left_pair[0], right_pair[1], precision=HIGHEST) + jnp.einsum(
        pattern, left_pair[1], right_pair[0], precision=HIGHEST
    )
    return (real_part, imag_part)


def remodulate(symbols):
    emitter_number, length = symbols.shape
    column_entries = 128
    increment_spacing = length // column_entries
    inphase_amplitude = (2 * (symbols % 8) - 7).astype(jnp.float32) / math.sqrt(42.0)
    quadrature_amplitude = (2 * (symbols // 8) - 7).astype(jnp.float32) / math.sqrt(42.0)
    subcarrier = jnp.arange(length, dtype=jnp.int32) - length // 2
    occupied_tones = (jnp.abs(subcarrier) <= (ACTIVE - 1) // 2).astype(jnp.float32)
    tone_symbols = (
        (inphase_amplitude * occupied_tones).reshape(
            emitter_number, increment_spacing, column_entries
        ),
        (quadrature_amplitude * occupied_tones).reshape(
            emitter_number, increment_spacing, column_entries
        ),
    )
    partial_result = complex_multiply_result(
        "mb,nbd->nmd",
        rotation_angle_grid(increment_spacing, increment_spacing, increment_spacing),
        tone_symbols,
    )
    twiddle = rotation_angle_grid(increment_spacing, column_entries, length)
    partial_result = (
        partial_result[0] * twiddle[0] - partial_result[1] * twiddle[1],
        partial_result[0] * twiddle[1] + partial_result[1] * twiddle[0],
    )
    frequency_spectrum = complex_multiply_result(
        "pho,oj->phj",
        partial_result,
        rotation_angle_grid(column_entries, column_entries, column_entries),
    )
    alternate = (1 - 2 * (jnp.arange(length, dtype=jnp.int32) % 2)).astype(jnp.float32) / math.sqrt(
        ACTIVE
    )
    real_part = (
        jnp.swapaxes(frequency_spectrum[0], 1, 2).reshape(emitter_number, length) * alternate
    )
    imag_part = (
        jnp.swapaxes(frequency_spectrum[1], 1, 2).reshape(emitter_number, length) * alternate
    )
    return jnp.stack([real_part, imag_part], axis=1).astype(jnp.bfloat16)


def lanes_of(shape):
    return lax.broadcasted_iota(jnp.int32, shape, len(shape) - 1)


def rows_of(shape):
    return lax.broadcasted_iota(jnp.int32, shape, len(shape) - 2)


def half_turn(block):
    return pltpu.roll(block, LANES // 2, 1)


def several(count, together, body):
    together = math.gcd(count, together)

    def step(i, carry):
        for t in range(together):
            carry = body(i * together + t, carry)
        return carry

    lax.fori_loop(0, count // together, step, 0)


def signal_matrix(re, im):
    low = lanes_of(re.shape) < LANES // 2
    turned_re, turned_im = half_turn(re), half_turn(im)
    return jnp.concatenate(
        [
            jnp.where(low, re, turned_im),
            jnp.where(low, turned_re, im),
            jnp.where(low, im, -turned_re),
            jnp.where(low, turned_im, -re),
        ],
        axis=0,
    ).astype(jnp.bfloat16)


def fold_lags(product):
    half = LANES // 2
    shape = (half, LANES)
    earlier = lanes_of(shape) % half < rows_of(shape)
    total = jnp.where(earlier, half_turn(product[:half]), product[half:])
    rows = half // 2
    while rows >= 8:
        total = total[:rows] + pltpu.roll(total[rows:], LANES - rows, 1)
        rows //= 2
    for step in (4, 2, 1):
        total = total + pltpu.roll(pltpu.roll(total, LANES - step, 1), 8 - step, 0)
    return total[:1]


def front_kernel(
    slots, delays, gains, x_ref, xp_ref, echo_ref, recv_ref, corr_ref, cross_ref, fq_ref, ft_ref
):
    window, _, rows, _ = x_ref.shape
    recv_count = echo_ref.shape[1]
    lane = lanes_of((rows, LANES))
    low = lane < LANES // 2

    def frame(i, carry):
        parts = []
        for c in range(2):
            x = x_ref[i, c]
            parts += [half_turn(jnp.where(low, x, xp_ref[i, c])), x]
        whole = jnp.concatenate(parts, axis=0)
        fq_ref[i] = whole.astype(jnp.bfloat16)
        ft_ref[i] = whole.T.astype(jnp.bfloat16)
        return carry

    lax.fori_loop(0, window, frame, 0)

    def pairs(j, carry):
        matrix = signal_matrix(x_ref[j, 0], x_ref[j, 1])
        for i in range(window):
            product = jnp.dot(ft_ref[i], matrix, preferred_element_type=jnp.float32)
            corr_ref[j, i : i + 1, :] = fold_lags(product)
        return carry

    lax.fori_loop(0, window, pairs, 0)

    def receiver(r, carry):
        re = jnp.zeros((rows, LANES), jnp.float32)
        im = jnp.zeros((rows, LANES), jnp.float32)
        for k in range(PER_RECV):
            s = slots[r, k]
            d = delays[r, k]
            g_re = gains[0, r, k]
            g_im = gains[1, r, k]
            wrapped = lane >= LANES - d
            y_re = pltpu.roll(jnp.where(wrapped, xp_ref[s, 0], x_ref[s, 0]), d, 1)
            y_im = pltpu.roll(jnp.where(wrapped, xp_ref[s, 1], x_ref[s, 1]), d, 1)
            re = re + (g_re * y_re - g_im * y_im)
            im = im + (g_re * y_im + g_im * y_re)
        re = (echo_ref[0, r].astype(jnp.float32) + re).astype(jnp.bfloat16)
        im = (echo_ref[1, r].astype(jnp.float32) + im).astype(jnp.bfloat16)
        recv_ref[0, r] = re
        recv_ref[1, r] = im
        matrix = signal_matrix(re.astype(jnp.float32), im.astype(jnp.float32))
        for k in range(PER_RECV):
            product = jnp.dot(ft_ref[slots[r, k]], matrix, preferred_element_type=jnp.float32)
            cross_ref[r, k : k + 1, :] = fold_lags(product)
        return carry

    several(recv_count, 2, receiver)


def back_kernel(slots, taps_ref, fq_ref, recv_ref, out_ref):
    recv_count, rows = recv_ref.shape[1:3]
    half = LANES // 2
    shape = (LANES, LANES)
    place = lanes_of(shape) % half
    row = rows_of(shape)
    valid = ((row < half) & (place < row)) | ((row >= half) & (place >= row - half))
    low = lanes_of((LANES, LANES)) < half
    low_half = lanes_of((rows, LANES)) < half

    def receiver(r, carry):
        total = jnp.zeros((4 * rows, LANES), jnp.float32)
        for k in range(PER_RECV):
            base = jnp.broadcast_to(taps_ref[r, k : k + 1, :], shape)
            band = pltpu.roll(base, half, 1, stride=1, stride_axis=0)
            band = jnp.where(valid, band, 0.0).astype(jnp.bfloat16)
            total = total + jnp.dot(
                fq_ref[slots[r, k]], band, preferred_element_type=jnp.float32
            )
        turned = half_turn(total[2 * rows :])
        both = total[: 2 * rows] + jnp.where(low, -turned, turned)
        first, second = both[:rows], both[rows:]
        re = jnp.where(low_half, first, half_turn(second))
        im = jnp.where(low_half, half_turn(first), second)
        out_ref[0, r] = (recv_ref[0, r].astype(jnp.float32) - re).astype(jnp.bfloat16)
        out_ref[1, r] = (recv_ref[1, r].astype(jnp.float32) - im).astype(jnp.bfloat16)
        return carry

    several(recv_count, 4, receiver)


def times_i(block):
    pieces = []
    for start in range(0, block.shape[1], LANES):
        turned = half_turn(block[:, start : start + LANES])
        pieces.append(jnp.where(lanes_of(turned.shape) < LANES // 2, -turned, turned))
    return jnp.concatenate(pieces, axis=1)


def complex_dot(left, right):
    return jnp.dot(left, right, precision=HIGHEST, preferred_element_type=jnp.float32)


def as_real(block):
    return jnp.concatenate([block, times_i(block)], axis=0)


def invert(blocks):
    size = blocks[0].shape[0]
    panel = 8
    shape = (panel, LANES)
    lane, row_id = lanes_of(shape), rows_of(shape)
    group = lanes_of(blocks[0].shape) % size // panel
    blocks = list(blocks)
    for start in range(0, size, panel):
        panels = [a[start : start + panel] for a in blocks]
        for t in range(panel):
            j = start + t
            for s, rows in enumerate(panels):
                col_re = jnp.broadcast_to(rows[:, j : j + 1], shape)
                col_im = jnp.broadcast_to(rows[:, size + j : size + j + 1], shape)
                pivot = 1.0 / col_re[t : t + 1]
                rest = jnp.where((lane == j) | (lane == size + j), 0.0, rows)
                row = jnp.where(lane[:1] == j, 1.0, rest[t : t + 1])
                turned = half_turn(row)
                row_i = jnp.where(lane[:1] < size, -turned, turned) * pivot
                row = row * pivot
                rest = rest - col_re * row - col_im * row_i
                panels[s] = jnp.where(row_id == t, row, rest)
        chosen = group == start // panel
        for s, (a, rows) in enumerate(zip(blocks, panels)):
            above = [jnp.zeros((start, LANES), jnp.float32)] if start > 0 else []
            left = size - panel - start
            below = [jnp.zeros((left, LANES), jnp.float32)] if left > 0 else []
            pieces = above + [rows] + below + above + [times_i(rows)] + below
            change = complex_dot(jnp.where(chosen, a, 0.0), jnp.concatenate(pieces, axis=0))
            rest = jnp.where(chosen, 0.0, a) - change
            above = [rest[:start]] if start > 0 else []
            below = [rest[start + panel :]] if left > 0 else []
            blocks[s] = jnp.concatenate(above + [rows] + below, axis=0)
    return blocks


def solve_kernel(slots, vr_ref, vi_ref, rhs_ref, out_ref, a_ref, d_ref):
    share = rhs_ref.shape[0]
    size = DELAYS
    window = math.isqrt(vr_ref.shape[0])
    shape = (size, LANES)
    lane, row_id = lanes_of(shape), rows_of(shape)
    low = lane < size
    unit = jnp.where(lane == row_id, jnp.float32(loading), 0.0)
    end = PER_RECV * LANES

    def build(index, carry):
        s, k = index // PER_RECV, index % PER_RECV
        start = pl.multiple_of(k * size, size)
        first = slots[s, k]
        for l in range(PER_RECV):
            at = first * window + slots[s, l]
            re = jnp.broadcast_to(vr_ref[at], shape)
            im = jnp.broadcast_to(vi_ref[at], shape)
            block = jnp.where(
                low,
                pltpu.roll(re, 0, 1, stride=1, stride_axis=0),
                pltpu.roll(im, size, 1, stride=1, stride_axis=0),
            )
            block = block + jnp.where(k == l, unit, 0.0)
            a_ref[s, pl.ds(start, size), l * LANES : (l + 1) * LANES] = block
        side = rhs_ref[s, pl.ds(start, size), :]
        a_ref[s, pl.ds(start, size), end : end + LANES] = jnp.where(
            lane == 0, side[:, 0:1], jnp.where(lane == size, side[:, 1:2], 0.0)
        )
        return carry

    lax.fori_loop(0, share * PER_RECV, build, 0)

    def eliminate(p, carry):
        at_row = pl.multiple_of(p * size, size)
        at_col = pl.multiple_of(p * LANES, LANES)
        blocks = [a_ref[s, pl.ds(at_row, size), pl.ds(at_col, LANES)] for s in range(share)]
        for s, block in enumerate(invert(blocks)):
            d_ref[s] = block
        for step in range(PER_RECV):

            @pl.when(p == step)
            def _():
                top, left = step * size, (step + 1) * LANES
                for s in range(share):
                    right = a_ref[s, top : top + size, left:]
                    scaled = complex_dot(d_ref[s], as_real(right))
                    a_ref[s, top : top + size, left:] = scaled
                    if step < PER_RECV - 1:
                        below = a_ref[s, top + size :, left - LANES : left]
                        a_ref[s, top + size :, left:] -= complex_dot(below, as_real(scaled))

        return carry

    lax.fori_loop(0, PER_RECV, eliminate, 0)
    for s in range(share):
        known = None
        for p in reversed(range(PER_RECV)):
            top, left = p * size, (p + 1) * LANES
            found = a_ref[s, top : top + size, end : end + LANES]
            if known is not None:
                found = found - complex_dot(a_ref[s, top : top + size, left:end], known)
            out_ref[s, top : top + size, :] = found
            found = as_real(found)
            known = found if known is None else jnp.concatenate([found, known], axis=0)


def kernel_call(body, outs, scalars, arrays, scratch=(), **params):
    spec_smem = pl.BlockSpec(memory_space=pltpu.SMEM)
    spec_vmem = pl.BlockSpec(memory_space=pltpu.VMEM)
    return pl.pallas_call(
        body,
        out_shape=outs,
        in_specs=[spec_smem] * len(scalars) + [spec_vmem] * len(arrays),
        out_specs=jax.tree.map(lambda _: spec_vmem, outs),
        scratch_shapes=list(scratch),
        compiler_params=pltpu.CompilerParams(vmem_limit_bytes=48 * MIB, **params),
    )(*scalars, *arrays)


def peer(offset):
    count = lax.axis_size("tm")
    return lax.rem(lax.axis_index("tm") + offset, count)


def greet():
    count = lax.axis_size("tm")
    barrier = pltpu.get_barrier_semaphore()
    for offset in range(1, count):
        pl.semaphore_signal(
            barrier,
            inc=1,
            device_id={"tm": peer(offset)},
            device_id_type=pl.DeviceIdType.MESH,
        )
    pl.semaphore_wait(barrier, count - 1)


def push(source, target, sends, arrivals, offset):
    copy = pltpu.make_async_remote_copy(
        src_ref=source,
        dst_ref=target,
        send_sem=sends.at[offset],
        recv_sem=arrivals.at[offset],
        device_id={"tm": peer(offset)},
        device_id_type=pl.DeviceIdType.MESH,
    )
    copy.start()
    return copy


def sum_kernel(
    corr_ref, cross_ref, corr_out, cross_out, corr_in, cross_in, s0, r0, s1, r1, s2, r2
):
    count, rows = corr_in.shape[:2]
    share = cross_in.shape[1]
    me = lax.axis_index("tm")
    own_rows = pl.ds(pl.multiple_of(me * rows, rows), rows)
    own_share = pl.ds(me * share, share)
    greet()
    copies = []
    for offset in range(1, count):
        to = peer(offset)
        their_rows = pl.ds(pl.multiple_of(to * rows, rows), rows)
        their_share = pl.ds(to * share, share)
        copies.append(push(corr_ref.at[their_rows], corr_in.at[offset], s0, r0, offset))
        copies.append(push(cross_ref.at[their_share], cross_in.at[offset], s1, r1, offset))
    for copy in copies[::2]:
        copy.wait()
    total = corr_ref[own_rows, :]
    for offset in range(1, count):
        total = total + corr_in[offset]
    corr_out[own_rows, :] = total
    spread = [
        push(corr_out.at[own_rows], corr_out.at[own_rows], s2, r2, offset)
        for offset in range(1, count)
    ]
    for copy in copies[1::2]:
        copy.wait()
    total = cross_ref[own_share]
    for offset in range(1, count):
        total = total + cross_in[offset]
    cross_out[...] = total
    for copy in spread:
        copy.wait()


def gather_kernel(in_ref, out_ref, sends, arrivals):
    count = out_ref.shape[0]
    me = lax.axis_index("tm")
    greet()
    copies = [push(in_ref, out_ref.at[me], sends, arrivals, o) for o in range(1, count)]
    out_ref[me] = in_ref[...]
    for copy in copies:
        copy.wait()


def window_sums(corr_part, cross_part):
    count = lax.axis_size("tm")
    shares = (cross_part.shape[0] // count,) + cross_part.shape[1:]
    flat = corr_part.reshape(-1, LANES)
    rows = flat.shape[0] // count
    corr, cross = kernel_call(
        sum_kernel,
        (
            jax.ShapeDtypeStruct(flat.shape, jnp.float32),
            jax.ShapeDtypeStruct(shares, jnp.float32),
        ),
        (),
        (flat, cross_part),
        (
            pltpu.VMEM((count, rows, LANES), jnp.float32),
            pltpu.VMEM((count,) + shares, jnp.float32),
        )
        + (pltpu.SemaphoreType.DMA((count,)),) * 6,
        collective_id=0,
        has_side_effects=True,
    )
    return corr.reshape(corr_part.shape), cross


def gathered_weights(solved):
    count = lax.axis_size("tm")
    return kernel_call(
        gather_kernel,
        jax.ShapeDtypeStruct((count,) + solved.shape, jnp.float32),
        (),
        (solved,),
        (pltpu.SemaphoreType.DMA((count,)),) * 2,
        collective_id=1,
        has_side_effects=True,
    )


def local(symbols, incidence, delays, gains, echoes):
    local_refs = remodulate(symbols)
    owned = local_refs.shape[0]
    length = local_refs.shape[2]
    rows = length // LANES
    taps_count = PER_RECV * DELAYS
    chan_count = lax.axis_size("chan")
    chan_index = lax.axis_index("chan")
    tm_count = lax.axis_size("tm")
    tm_index = lax.axis_index("tm")
    window_count = 2 * owned
    recv_count = echoes.shape[1]
    following = passed_along(local_refs, "chan", -1)
    window = jnp.concatenate([local_refs, following], axis=0)
    previous = from_behind(window[:, :, length - DELAYS :], "tm", 1)
    previous = jnp.pad(previous, ((0, 0), (0, 0), (LANES - DELAYS, 0)))[:, :, None, :]
    x = window.reshape(window_count, 2, rows, LANES)
    xp = jnp.concatenate([previous, x[:, :, :-1]], axis=2).astype(jnp.float32)
    x = x.astype(jnp.float32)
    owner_chan = incidence // owned
    slot = (owner_chan - chan_index) % chan_count * owned + incidence % owned
    received, corr_part, cross_part, frames = kernel_call(
        front_kernel,
        (
            jax.ShapeDtypeStruct((2, recv_count, rows, LANES), jnp.bfloat16),
            jax.ShapeDtypeStruct((window_count, window_count, LANES), jnp.float32),
            jax.ShapeDtypeStruct((recv_count, PER_RECV, LANES), jnp.float32),
            jax.ShapeDtypeStruct((window_count, 4 * rows, LANES), jnp.bfloat16),
        ),
        (slot, delays, gains),
        (x, xp, echoes.reshape(2, recv_count, rows, LANES)),
        (pltpu.VMEM((window_count, LANES, 4 * rows), jnp.bfloat16),),
    )
    share = recv_count // tm_count
    scale = 1.0 / (length * tm_count)
    corr, cross = window_sums(corr_part, cross_part)
    corr = corr * scale
    cross = cross * scale
    mine = lax.dynamic_slice_in_dim(slot, tm_index * share, share, 0)
    swapped = jnp.swapaxes(corr, 0, 1)
    gap = jnp.zeros(corr.shape[:2] + (1,), jnp.float32)

    def diagonals(ahead, behind, sign):
        line = jnp.concatenate(
            [ahead[..., :1], sign * behind[..., 1:], gap, jnp.flip(ahead[..., 1:], axis=-1)], axis=-1
        )
        return line.reshape(window_count * window_count, 1, LANES)

    vr = diagonals(swapped[..., :DELAYS], corr[..., :DELAYS], 1.0)
    vi = diagonals(swapped[..., DELAYS:], corr[..., DELAYS:], -1.0)
    rhs = cross.reshape(share, PER_RECV, 2, DELAYS).swapaxes(2, 3).reshape(share, taps_count, 2)
    solved = kernel_call(
        solve_kernel,
        jax.ShapeDtypeStruct((share, taps_count, LANES), jnp.float32),
        (mine,),
        (vr, vi, rhs),
        (
            pltpu.VMEM((share, taps_count, (PER_RECV + 1) * LANES), jnp.float32),
            pltpu.VMEM((share, DELAYS, LANES), jnp.float32),
        ),
    )
    local_weights = jnp.stack([solved[:, :, 0], solved[:, :, DELAYS]], axis=1)
    gathered = gathered_weights(local_weights.reshape(share * 2, taps_count))
    gathered = gathered.reshape(recv_count, 2, taps_count)
    weights = jnp.swapaxes(gathered, 0, 1)
    taps = gathered.astype(jnp.bfloat16).astype(jnp.float32)
    taps = taps.reshape(recv_count, 2, PER_RECV, DELAYS).swapaxes(1, 2)
    taps = taps.reshape(recv_count, PER_RECV, LANES)
    cancelled = kernel_call(
        back_kernel,
        jax.ShapeDtypeStruct((2, recv_count, rows, LANES), jnp.bfloat16),
        (slot,),
        (taps, frames, received),
    )
    return (cancelled.reshape(2, recv_count, length), weights)


def solution(mesh):
    in_specs = (
        P("chan", "tm"),
        P("chan", None),
        P("chan", None),
        P(None, "chan", None),
        P(None, "chan", "tm"),
    )
    out_specs = (P(None, "chan", "tm"), P(None, "chan", None))
    return jax.shard_map(local, mesh=mesh, in_specs=in_specs, out_specs=out_specs, check_vma=False)
```

```python
import math

import jax
import jax.numpy as jnp
from jax import lax
from jax.experimental import pallas as pl
from jax.experimental.pallas import tpu as pltpu
from jax.sharding import PartitionSpec as P

ACTIVE = 6817
DELAYS = 64
PER_RECV = 6


loading = 0.1
LANES = 128
MIB = 2**20
HIGHEST = lax.Precision.HIGHEST


def passed_along(array, axis, by):
    peers = lax.axis_size(axis)
    return lax.ppermute(array, axis, [(i, (i + by) % peers) for i in range(peers)])


def from_behind(block, axis, distance):
    devices = range(lax.axis_size(axis))
    route = [(i - distance, i) for i in devices if i - distance in devices]
    return lax.ppermute(block, axis, route)


def rotation_angle_grid(row_count, col_count, period):
    product = (
        jnp.arange(row_count, dtype=jnp.int32)[:, None]
        * jnp.arange(col_count, dtype=jnp.int32)[None, :]
    )
    phases = (product % period).astype(jnp.float32) * (2.0 * math.pi / period)
    return (jnp.cos(phases), jnp.sin(phases))


def complex_multiply_result(pattern, left_pair, right_pair):
    real_part = jnp.einsum(pattern, left_pair[0], right_pair[0], precision=HIGHEST) - jnp.einsum(
        pattern, left_pair[1], right_pair[1], precision=HIGHEST
    )
    imag_part = jnp.einsum(pattern, left_pair[0], right_pair[1], precision=HIGHEST) + jnp.einsum(
        pattern, left_pair[1], right_pair[0], precision=HIGHEST
    )
    return (real_part, imag_part)


def remodulate(symbols):
    emitter_number, length = symbols.shape
    column_entries = 128
    increment_spacing = length // column_entries
    inphase_amplitude = (2 * (symbols % 8) - 7).astype(jnp.float32) / math.sqrt(42.0)
    quadrature_amplitude = (2 * (symbols // 8) - 7).astype(jnp.float32) / math.sqrt(42.0)
    subcarrier = jnp.arange(length, dtype=jnp.int32) - length // 2
    occupied_tones = (jnp.abs(subcarrier) <= (ACTIVE - 1) // 2).astype(jnp.float32)
    tone_symbols = (
        (inphase_amplitude * occupied_tones).reshape(
            emitter_number, increment_spacing, column_entries
        ),
        (quadrature_amplitude * occupied_tones).reshape(
            emitter_number, increment_spacing, column_entries
        ),
    )
    partial_result = complex_multiply_result(
        "mb,nbd->nmd",
        rotation_angle_grid(increment_spacing, increment_spacing, increment_spacing),
        tone_symbols,
    )
    twiddle = rotation_angle_grid(increment_spacing, column_entries, length)
    partial_result = (
        partial_result[0] * twiddle[0] - partial_result[1] * twiddle[1],
        partial_result[0] * twiddle[1] + partial_result[1] * twiddle[0],
    )
    frequency_spectrum = complex_multiply_result(
        "pho,oj->phj",
        partial_result,
        rotation_angle_grid(column_entries, column_entries, column_entries),
    )
    alternate = (1 - 2 * (jnp.arange(length, dtype=jnp.int32) % 2)).astype(jnp.float32) / math.sqrt(
        ACTIVE
    )
    real_part = (
        jnp.swapaxes(frequency_spectrum[0], 1, 2).reshape(emitter_number, length) * alternate
    )
    imag_part = (
        jnp.swapaxes(frequency_spectrum[1], 1, 2).reshape(emitter_number, length) * alternate
    )
    return jnp.stack([real_part, imag_part], axis=1).astype(jnp.bfloat16)


def lanes_of(shape):
    return lax.broadcasted_iota(jnp.int32, shape, len(shape) - 1)


def rows_of(shape):
    return lax.broadcasted_iota(jnp.int32, shape, len(shape) - 2)


def half_turn(block):
    return pltpu.roll(block, LANES // 2, 1)


def several(count, together, body):
    together = math.gcd(count, together)

    def step(i, carry):
        for t in range(together):
            carry = body(i * together + t, carry)
        return carry

    lax.fori_loop(0, count // together, step, 0)


def signal_matrix(re, im):
    low = lanes_of(re.shape) < LANES // 2
    turned_re, turned_im = half_turn(re), half_turn(im)
    return jnp.concatenate(
        [
            jnp.where(low, re, turned_im),
            jnp.where(low, turned_re, im),
            jnp.where(low, im, -turned_re),
            jnp.where(low, turned_im, -re),
        ],
        axis=0,
    ).astype(jnp.bfloat16)


def fold_lags(product):
    half = LANES // 2
    shape = (half, LANES)
    earlier = lanes_of(shape) % half < rows_of(shape)
    total = jnp.where(earlier, half_turn(product[:half]), product[half:])
    rows = half // 2
    while rows >= 8:
        total = total[:rows] + pltpu.roll(total[rows:], LANES - rows, 1)
        rows //= 2
    for step in (4, 2, 1):
        total = total + pltpu.roll(pltpu.roll(total, LANES - step, 1), 8 - step, 0)
    return total[:1]


def front_kernel(
    slots, delays, gains, x_ref, xp_ref, echo_ref, recv_ref, corr_ref, cross_ref, fq_ref, ft_ref
):
    window, _, rows, _ = x_ref.shape
    recv_count = echo_ref.shape[1]
    lane = lanes_of((rows, LANES))
    low = lane < LANES // 2

    def frame(i, carry):
        parts = []
        for c in range(2):
            x = x_ref[i, c]
            parts += [half_turn(jnp.where(low, x, xp_ref[i, c])), x]
        whole = jnp.concatenate(parts, axis=0)
        fq_ref[i] = whole.astype(jnp.bfloat16)
        ft_ref[i] = whole.T.astype(jnp.bfloat16)
        return carry

    lax.fori_loop(0, window, frame, 0)

    def pairs(j, carry):
        matrix = signal_matrix(x_ref[j, 0], x_ref[j, 1])
        for i in range(window):
            product = jnp.dot(ft_ref[i], matrix, preferred_element_type=jnp.float32)
            corr_ref[j, i : i + 1, :] = fold_lags(product)
        return carry

    lax.fori_loop(0, window, pairs, 0)

    def receiver(r, carry):
        re = jnp.zeros((rows, LANES), jnp.float32)
        im = jnp.zeros((rows, LANES), jnp.float32)
        for k in range(PER_RECV):
            s = slots[r, k]
            d = delays[r, k]
            g_re = gains[0, r, k]
            g_im = gains[1, r, k]
            wrapped = lane >= LANES - d
            y_re = pltpu.roll(jnp.where(wrapped, xp_ref[s, 0], x_ref[s, 0]), d, 1)
            y_im = pltpu.roll(jnp.where(wrapped, xp_ref[s, 1], x_ref[s, 1]), d, 1)
            re = re + (g_re * y_re - g_im * y_im)
            im = im + (g_re * y_im + g_im * y_re)
        re = (echo_ref[0, r].astype(jnp.float32) + re).astype(jnp.bfloat16)
        im = (echo_ref[1, r].astype(jnp.float32) + im).astype(jnp.bfloat16)
        recv_ref[0, r] = re
        recv_ref[1, r] = im
        matrix = signal_matrix(re.astype(jnp.float32), im.astype(jnp.float32))
        for k in range(PER_RECV):
            product = jnp.dot(ft_ref[slots[r, k]], matrix, preferred_element_type=jnp.float32)
            cross_ref[r, k : k + 1, :] = fold_lags(product)
        return carry

    several(recv_count, 4, receiver)


def back_kernel(slots, taps_ref, fq_ref, recv_ref, out_ref):
    recv_count, rows = recv_ref.shape[1:3]
    half = LANES // 2
    shape = (LANES, LANES)
    place = lanes_of(shape) % half
    row = rows_of(shape)
    valid = ((row < half) & (place < row)) | ((row >= half) & (place >= row - half))
    low = lanes_of((LANES, LANES)) < half
    low_half = lanes_of((rows, LANES)) < half

    def receiver(r, carry):
        total = jnp.zeros((4 * rows, LANES), jnp.float32)
        for k in range(PER_RECV):
            base = jnp.broadcast_to(taps_ref[r, k : k + 1, :], shape)
            band = pltpu.roll(base, half, 1, stride=1, stride_axis=0)
            band = jnp.where(valid, band, 0.0).astype(jnp.bfloat16)
            total = total + jnp.dot(
                fq_ref[slots[r, k]], band, preferred_element_type=jnp.float32
            )
        turned = half_turn(total[2 * rows :])
        both = total[: 2 * rows] + jnp.where(low, -turned, turned)
        first, second = both[:rows], both[rows:]
        re = jnp.where(low_half, first, half_turn(second))
        im = jnp.where(low_half, half_turn(first), second)
        out_ref[0, r] = (recv_ref[0, r].astype(jnp.float32) - re).astype(jnp.bfloat16)
        out_ref[1, r] = (recv_ref[1, r].astype(jnp.float32) - im).astype(jnp.bfloat16)
        return carry

    several(recv_count, 4, receiver)


def times_i(block):
    pieces = []
    for start in range(0, block.shape[1], LANES):
        turned = half_turn(block[:, start : start + LANES])
        pieces.append(jnp.where(lanes_of(turned.shape) < LANES // 2, -turned, turned))
    return jnp.concatenate(pieces, axis=1)


def complex_dot(left, right):
    return jnp.dot(left, right, precision=HIGHEST, preferred_element_type=jnp.float32)


def as_real(block):
    return jnp.concatenate([block, times_i(block)], axis=0)


def three_parts(value):
    parts = []
    for _ in range(3):
        part = value.astype(jnp.bfloat16).astype(jnp.float32)
        parts.append(part)
        value = value - part
    return parts


def panel_product(left, rows, place, start):
    panel = rows.shape[0]
    for shift in (panel, 2 * panel, 4 * panel):
        left = left + pltpu.roll(left, shift, 1)
    high, middle, low = three_parts(left)
    left = jnp.where(place < 3, high, jnp.where(place < 5, middle, low))
    left = jnp.where(place < 6, left, 0.0).astype(jnp.bfloat16)
    gap = jnp.zeros_like(rows)
    pieces = []
    for block in (rows, times_i(rows)):
        p, q, r = three_parts(block)
        pieces += [p, q, r, p, q, p, gap, gap]
    turn = start // panel
    pieces = pieces[len(pieces) - turn :] + pieces[: len(pieces) - turn]
    right = jnp.concatenate(pieces, axis=0).astype(jnp.bfloat16)
    return jnp.dot(left, right, preferred_element_type=jnp.float32)


def invert(blocks):
    size = blocks[0].shape[0]
    panel = 8
    shape = (panel, LANES)
    lane, row_id = lanes_of(shape), rows_of(shape)
    group = lanes_of(blocks[0].shape) % size // panel
    blocks = list(blocks)
    for start in range(0, size, panel):
        panels = [a[start : start + panel] for a in blocks]
        for t in range(panel):
            j = start + t
            for s, rows in enumerate(panels):
                col_re = jnp.broadcast_to(rows[:, j : j + 1], shape)
                col_im = jnp.broadcast_to(rows[:, size + j : size + j + 1], shape)
                pivot = 1.0 / col_re[t : t + 1]
                rest = jnp.where((lane == j) | (lane == size + j), 0.0, rows)
                row = jnp.where(lane[:1] == j, 1.0, rest[t : t + 1])
                turned = half_turn(row)
                row_i = jnp.where(lane[:1] < size, -turned, turned) * pivot
                row = row * pivot
                rest = rest - col_re * row - col_im * row_i
                panels[s] = jnp.where(row_id == t, row, rest)
        chosen = group == start // panel
        place = (lanes_of(blocks[0].shape) + (LANES - start)) % size // panel
        for s, (a, rows) in enumerate(zip(blocks, panels)):
            left = size - panel - start
            change = panel_product(jnp.where(chosen, a, 0.0), rows, place, start)
            rest = jnp.where(chosen, 0.0, a) - change
            above = [rest[:start]] if start > 0 else []
            below = [rest[start + panel :]] if left > 0 else []
            blocks[s] = jnp.concatenate(above + [rows] + below, axis=0)
    return blocks


def solve_kernel(slots, vr_ref, vi_ref, rhs_ref, out_ref, a_ref, d_ref):
    share = rhs_ref.shape[0]
    size = DELAYS
    window = math.isqrt(vr_ref.shape[0])
    shape = (size, LANES)
    lane, row_id = lanes_of(shape), rows_of(shape)
    low = lane < size
    unit = jnp.where(lane == row_id, jnp.float32(loading), 0.0)
    end = PER_RECV * LANES

    def build(index, carry):
        s, k = index // PER_RECV, index % PER_RECV
        start = pl.multiple_of(k * size, size)
        first = slots[s, k]
        for l in range(PER_RECV):
            at = first * window + slots[s, l]
            re = jnp.broadcast_to(vr_ref[at], shape)
            im = jnp.broadcast_to(vi_ref[at], shape)
            block = jnp.where(
                low,
                pltpu.roll(re, 0, 1, stride=1, stride_axis=0),
                pltpu.roll(im, size, 1, stride=1, stride_axis=0),
            )
            block = block + jnp.where(k == l, unit, 0.0)
            a_ref[s, pl.ds(start, size), l * LANES : (l + 1) * LANES] = block
        side = rhs_ref[s, pl.ds(start, size), :]
        a_ref[s, pl.ds(start, size), end : end + LANES] = jnp.where(
            lane == 0, side[:, 0:1], jnp.where(lane == size, side[:, 1:2], 0.0)
        )
        return carry

    lax.fori_loop(0, share * PER_RECV, build, 0)

    def eliminate(p, carry):
        at_row = pl.multiple_of(p * size, size)
        at_col = pl.multiple_of(p * LANES, LANES)
        blocks = [a_ref[s, pl.ds(at_row, size), pl.ds(at_col, LANES)] for s in range(share)]
        for s, block in enumerate(invert(blocks)):
            d_ref[s] = block
        for step in range(PER_RECV):

            @pl.when(p == step)
            def _():
                top, left = step * size, (step + 1) * LANES
                for s in range(share):
                    right = a_ref[s, top : top + size, left:]
                    scaled = complex_dot(d_ref[s], as_real(right))
                    a_ref[s, top : top + size, left:] = scaled
                    if step < PER_RECV - 1:
                        below = a_ref[s, top + size :, left - LANES : left]
                        a_ref[s, top + size :, left:] -= complex_dot(below, as_real(scaled))

        return carry

    lax.fori_loop(0, PER_RECV, eliminate, 0)
    for s in range(share):
        known = None
        for p in reversed(range(PER_RECV)):
            top, left = p * size, (p + 1) * LANES
            found = a_ref[s, top : top + size, end : end + LANES]
            if known is not None:
                found = found - complex_dot(a_ref[s, top : top + size, left:end], known)
            out_ref[s, top : top + size, :] = found
            found = as_real(found)
            known = found if known is None else jnp.concatenate([found, known], axis=0)


def kernel_call(body, outs, scalars, arrays, scratch=(), **params):
    spec_smem = pl.BlockSpec(memory_space=pltpu.SMEM)
    spec_vmem = pl.BlockSpec(memory_space=pltpu.VMEM)
    return pl.pallas_call(
        body,
        out_shape=outs,
        in_specs=[spec_smem] * len(scalars) + [spec_vmem] * len(arrays),
        out_specs=jax.tree.map(lambda _: spec_vmem, outs),
        scratch_shapes=list(scratch),
        compiler_params=pltpu.CompilerParams(vmem_limit_bytes=48 * MIB, **params),
    )(*scalars, *arrays)


def peer(offset):
    count = lax.axis_size("tm")
    return lax.rem(lax.axis_index("tm") + offset, count)


def greet():
    count = lax.axis_size("tm")
    barrier = pltpu.get_barrier_semaphore()
    for offset in range(1, count):
        pl.semaphore_signal(
            barrier,
            inc=1,
            device_id={"tm": peer(offset)},
            device_id_type=pl.DeviceIdType.MESH,
        )
    pl.semaphore_wait(barrier, count - 1)


def push(source, target, sends, arrivals, offset):
    copy = pltpu.make_async_remote_copy(
        src_ref=source,
        dst_ref=target,
        send_sem=sends.at[offset],
        recv_sem=arrivals.at[offset],
        device_id={"tm": peer(offset)},
        device_id_type=pl.DeviceIdType.MESH,
    )
    copy.start()
    return copy


def sum_kernel(
    corr_ref, cross_ref, corr_out, cross_out, corr_in, cross_in, s0, r0, s1, r1, s2, r2
):
    count, rows = corr_in.shape[:2]
    share = cross_in.shape[1]
    me = lax.axis_index("tm")
    own_rows = pl.ds(pl.multiple_of(me * rows, rows), rows)
    own_share = pl.ds(me * share, share)
    greet()
    copies = []
    for offset in range(1, count):
        to = peer(offset)
        their_rows = pl.ds(pl.multiple_of(to * rows, rows), rows)
        their_share = pl.ds(to * share, share)
        copies.append(push(corr_ref.at[their_rows], corr_in.at[offset], s0, r0, offset))
        copies.append(push(cross_ref.at[their_share], cross_in.at[offset], s1, r1, offset))
    for copy in copies[::2]:
        copy.wait()
    total = corr_ref[own_rows, :]
    for offset in range(1, count):
        total = total + corr_in[offset]
    corr_out[own_rows, :] = total
    spread = [
        push(corr_out.at[own_rows], corr_out.at[own_rows], s2, r2, offset)
        for offset in range(1, count)
    ]
    for copy in copies[1::2]:
        copy.wait()
    total = cross_ref[own_share]
    for offset in range(1, count):
        total = total + cross_in[offset]
    cross_out[...] = total
    for copy in spread:
        copy.wait()


def gather_kernel(in_ref, out_ref, sends, arrivals):
    count = out_ref.shape[0]
    me = lax.axis_index("tm")
    greet()
    copies = [push(in_ref, out_ref.at[me], sends, arrivals, o) for o in range(1, count)]
    out_ref[me] = in_ref[...]
    for copy in copies:
        copy.wait()


def window_sums(corr_part, cross_part):
    count = lax.axis_size("tm")
    shares = (cross_part.shape[0] // count,) + cross_part.shape[1:]
    flat = corr_part.reshape(-1, LANES)
    rows = flat.shape[0] // count
    corr, cross = kernel_call(
        sum_kernel,
        (
            jax.ShapeDtypeStruct(flat.shape, jnp.float32),
            jax.ShapeDtypeStruct(shares, jnp.float32),
        ),
        (),
        (flat, cross_part),
        (
            pltpu.VMEM((count, rows, LANES), jnp.float32),
            pltpu.VMEM((count,) + shares, jnp.float32),
        )
        + (pltpu.SemaphoreType.DMA((count,)),) * 6,
        collective_id=0,
        has_side_effects=True,
    )
    return corr.reshape(corr_part.shape), cross


def gathered_weights(solved):
    count = lax.axis_size("tm")
    return kernel_call(
        gather_kernel,
        jax.ShapeDtypeStruct((count,) + solved.shape, jnp.float32),
        (),
        (solved,),
        (pltpu.SemaphoreType.DMA((count,)),) * 2,
        collective_id=1,
        has_side_effects=True,
    )


def local(symbols, incidence, delays, gains, echoes):
    local_refs = remodulate(symbols)
    owned = local_refs.shape[0]
    length = local_refs.shape[2]
    rows = length // LANES
    taps_count = PER_RECV * DELAYS
    chan_count = lax.axis_size("chan")
    chan_index = lax.axis_index("chan")
    tm_count = lax.axis_size("tm")
    tm_index = lax.axis_index("tm")
    window_count = 2 * owned
    recv_count = echoes.shape[1]
    tails = local_refs[:, :, length - DELAYS :]
    following = passed_along(local_refs, "chan", -1)
    window = jnp.concatenate([local_refs, following], axis=0)
    route = [
        (c * tm_count + t, (c - 1) % chan_count * tm_count + t + 1)
        for c in range(chan_count)
        for t in range(tm_count - 1)
    ]
    previous = jnp.concatenate(
        [from_behind(tails, "tm", 1), lax.ppermute(tails, ("chan", "tm"), route)], axis=0
    )
    previous = jnp.pad(previous, ((0, 0), (0, 0), (LANES - DELAYS, 0)))[:, :, None, :]
    x = window.reshape(window_count, 2, rows, LANES)
    xp = jnp.concatenate([previous, x[:, :, :-1]], axis=2).astype(jnp.float32)
    x = x.astype(jnp.float32)
    owner_chan = incidence // owned
    slot = (owner_chan - chan_index) % chan_count * owned + incidence % owned
    received, corr_part, cross_part, frames = kernel_call(
        front_kernel,
        (
            jax.ShapeDtypeStruct((2, recv_count, rows, LANES), jnp.bfloat16),
            jax.ShapeDtypeStruct((window_count, window_count, LANES), jnp.float32),
            jax.ShapeDtypeStruct((recv_count, PER_RECV, LANES), jnp.float32),
            jax.ShapeDtypeStruct((window_count, 4 * rows, LANES), jnp.bfloat16),
        ),
        (slot, delays, gains),
        (x, xp, echoes.reshape(2, recv_count, rows, LANES)),
        (pltpu.VMEM((window_count, LANES, 4 * rows), jnp.bfloat16),),
    )
    share = recv_count // tm_count
    scale = 1.0 / (length * tm_count)
    corr, cross = window_sums(corr_part, cross_part)
    corr = corr * scale
    cross = cross * scale
    mine = lax.dynamic_slice_in_dim(slot, tm_index * share, share, 0)
    swapped = jnp.swapaxes(corr, 0, 1)
    gap = jnp.zeros(corr.shape[:2] + (1,), jnp.float32)

    def diagonals(ahead, behind, sign):
        line = jnp.concatenate(
            [ahead[..., :1], sign * behind[..., 1:], gap, jnp.flip(ahead[..., 1:], axis=-1)], axis=-1
        )
        return line.reshape(window_count * window_count, 1, LANES)

    vr = diagonals(swapped[..., :DELAYS], corr[..., :DELAYS], 1.0)
    vi = diagonals(swapped[..., DELAYS:], corr[..., DELAYS:], -1.0)
    rhs = cross.reshape(share, PER_RECV, 2, DELAYS).swapaxes(2, 3).reshape(share, taps_count, 2)
    solved = kernel_call(
        solve_kernel,
        jax.ShapeDtypeStruct((share, taps_count, LANES), jnp.float32),
        (mine,),
        (vr, vi, rhs),
        (
            pltpu.VMEM((share, taps_count, (PER_RECV + 1) * LANES), jnp.float32),
            pltpu.VMEM((share, DELAYS, LANES), jnp.float32),
        ),
    )
    local_weights = jnp.stack([solved[:, :, 0], solved[:, :, DELAYS]], axis=1)
    gathered = gathered_weights(local_weights.reshape(share * 2, taps_count))
    gathered = gathered.reshape(recv_count, 2, taps_count)
    weights = jnp.swapaxes(gathered, 0, 1)
    taps = gathered.astype(jnp.bfloat16).astype(jnp.float32)
    taps = taps.reshape(recv_count, 2, PER_RECV, DELAYS).swapaxes(1, 2)
    taps = taps.reshape(recv_count, PER_RECV, LANES)
    cancelled = kernel_call(
        back_kernel,
        jax.ShapeDtypeStruct((2, recv_count, rows, LANES), jnp.bfloat16),
        (slot,),
        (taps, frames, received),
    )
    return (cancelled.reshape(2, recv_count, length), weights)


def solution(mesh):
    in_specs = (
        P("chan", "tm"),
        P("chan", None),
        P("chan", None),
        P(None, "chan", None),
        P(None, "chan", "tm"),
    )
    out_specs = (P(None, "chan", "tm"), P(None, "chan", None))
    return jax.shard_map(local, mesh=mesh, in_specs=in_specs, out_specs=out_specs, check_vma=False)
```

```python
import math

import jax
import jax.numpy as jnp
from jax import lax
from jax.experimental import pallas as pl
from jax.experimental.pallas import tpu as pltpu
from jax.sharding import PartitionSpec as P

ACTIVE = 6817
DELAYS = 64
PER_RECV = 6


loading = 0.1
LANES = 128
MIB = 2**20
HIGHEST = lax.Precision.HIGHEST


def passed_along(array, axis, by):
    peers = lax.axis_size(axis)
    return lax.ppermute(array, axis, [(i, (i + by) % peers) for i in range(peers)])


def from_behind(block, axis, distance):
    devices = range(lax.axis_size(axis))
    route = [(i - distance, i) for i in devices if i - distance in devices]
    return lax.ppermute(block, axis, route)


def rotation_angle_grid(row_count, col_count, period):
    product = (
        jnp.arange(row_count, dtype=jnp.int32)[:, None]
        * jnp.arange(col_count, dtype=jnp.int32)[None, :]
    )
    phases = (product % period).astype(jnp.float32) * (2.0 * math.pi / period)
    return (jnp.cos(phases), jnp.sin(phases))


def complex_multiply_result(pattern, left_pair, right_pair):
    real_part = jnp.einsum(pattern, left_pair[0], right_pair[0], precision=HIGHEST) - jnp.einsum(
        pattern, left_pair[1], right_pair[1], precision=HIGHEST
    )
    imag_part = jnp.einsum(pattern, left_pair[0], right_pair[1], precision=HIGHEST) + jnp.einsum(
        pattern, left_pair[1], right_pair[0], precision=HIGHEST
    )
    return (real_part, imag_part)


def remodulate(symbols):
    emitter_number, length = symbols.shape
    column_entries = 128
    increment_spacing = length // column_entries
    inphase_amplitude = (2 * (symbols % 8) - 7).astype(jnp.float32) / math.sqrt(42.0)
    quadrature_amplitude = (2 * (symbols // 8) - 7).astype(jnp.float32) / math.sqrt(42.0)
    subcarrier = jnp.arange(length, dtype=jnp.int32) - length // 2
    occupied_tones = (jnp.abs(subcarrier) <= (ACTIVE - 1) // 2).astype(jnp.float32)
    tone_symbols = (
        (inphase_amplitude * occupied_tones).reshape(
            emitter_number, increment_spacing, column_entries
        ),
        (quadrature_amplitude * occupied_tones).reshape(
            emitter_number, increment_spacing, column_entries
        ),
    )
    partial_result = complex_multiply_result(
        "mb,nbd->nmd",
        rotation_angle_grid(increment_spacing, increment_spacing, increment_spacing),
        tone_symbols,
    )
    twiddle = rotation_angle_grid(increment_spacing, column_entries, length)
    partial_result = (
        partial_result[0] * twiddle[0] - partial_result[1] * twiddle[1],
        partial_result[0] * twiddle[1] + partial_result[1] * twiddle[0],
    )
    frequency_spectrum = complex_multiply_result(
        "pho,oj->phj",
        partial_result,
        rotation_angle_grid(column_entries, column_entries, column_entries),
    )
    alternate = (1 - 2 * (jnp.arange(length, dtype=jnp.int32) % 2)).astype(jnp.float32) / math.sqrt(
        ACTIVE
    )
    real_part = (
        jnp.swapaxes(frequency_spectrum[0], 1, 2).reshape(emitter_number, length) * alternate
    )
    imag_part = (
        jnp.swapaxes(frequency_spectrum[1], 1, 2).reshape(emitter_number, length) * alternate
    )
    return jnp.stack([real_part, imag_part], axis=1).astype(jnp.bfloat16)


def lanes_of(shape):
    return lax.broadcasted_iota(jnp.int32, shape, len(shape) - 1)


def rows_of(shape):
    return lax.broadcasted_iota(jnp.int32, shape, len(shape) - 2)


def half_turn(block):
    return pltpu.roll(block, LANES // 2, 1)


def several(count, together, body):
    together = math.gcd(count, together)

    def step(i, carry):
        for t in range(together):
            carry = body(i * together + t, carry)
        return carry

    lax.fori_loop(0, count // together, step, 0)


def signal_matrix(re, im):
    low = lanes_of(re.shape) < LANES // 2
    turned_re, turned_im = half_turn(re), half_turn(im)
    return jnp.concatenate(
        [
            jnp.where(low, re, turned_im),
            jnp.where(low, turned_re, im),
            jnp.where(low, im, -turned_re),
            jnp.where(low, turned_im, -re),
        ],
        axis=0,
    ).astype(jnp.bfloat16)


def fold_lags(product):
    half = LANES // 2
    shape = (half, LANES)
    earlier = lanes_of(shape) % half < rows_of(shape)
    total = jnp.where(earlier, half_turn(product[:half]), product[half:])
    rows = half // 2
    while rows >= 8:
        total = total[:rows] + pltpu.roll(total[rows:], LANES - rows, 1)
        rows //= 2
    for step in (4, 2, 1):
        total = total + pltpu.roll(pltpu.roll(total, LANES - step, 1), 8 - step, 0)
    return total[:1]


def front_kernel(
    slots, delays, gains, x_ref, xp_ref, echo_ref, recv_ref, corr_ref, cross_ref, fq_ref, ft_ref
):
    window, _, rows, _ = x_ref.shape
    recv_count = echo_ref.shape[1]
    lane = lanes_of((rows, LANES))
    low = lane < LANES // 2

    def frame(i, carry):
        parts = []
        for c in range(2):
            x = x_ref[i, c]
            parts += [half_turn(jnp.where(low, x, xp_ref[i, c])), x]
        whole = jnp.concatenate(parts, axis=0)
        fq_ref[i] = whole.astype(jnp.bfloat16)
        ft_ref[i] = whole.T.astype(jnp.bfloat16)
        return carry

    lax.fori_loop(0, window, frame, 0)

    def pairs(j, carry):
        matrix = signal_matrix(x_ref[j, 0], x_ref[j, 1])
        for i in range(window):
            product = jnp.dot(ft_ref[i], matrix, preferred_element_type=jnp.float32)
            corr_ref[j, i : i + 1, :] = fold_lags(product)
        return carry

    lax.fori_loop(0, window, pairs, 0)

    def receiver(r, carry):
        re = jnp.zeros((rows, LANES), jnp.float32)
        im = jnp.zeros((rows, LANES), jnp.float32)
        for k in range(PER_RECV):
            s = slots[r, k]
            d = delays[r, k]
            g_re = gains[0, r, k]
            g_im = gains[1, r, k]
            wrapped = lane >= LANES - d
            y_re = pltpu.roll(jnp.where(wrapped, xp_ref[s, 0], x_ref[s, 0]), d, 1)
            y_im = pltpu.roll(jnp.where(wrapped, xp_ref[s, 1], x_ref[s, 1]), d, 1)
            re = re + (g_re * y_re - g_im * y_im)
            im = im + (g_re * y_im + g_im * y_re)
        re = (echo_ref[0, r].astype(jnp.float32) + re).astype(jnp.bfloat16)
        im = (echo_ref[1, r].astype(jnp.float32) + im).astype(jnp.bfloat16)
        recv_ref[0, r] = re
        recv_ref[1, r] = im
        matrix = signal_matrix(re.astype(jnp.float32), im.astype(jnp.float32))
        for k in range(PER_RECV):
            product = jnp.dot(ft_ref[slots[r, k]], matrix, preferred_element_type=jnp.float32)
            cross_ref[r, k : k + 1, :] = fold_lags(product)
        return carry

    several(recv_count, 2, receiver)


def back_kernel(slots, taps_ref, fq_ref, recv_ref, out_ref):
    recv_count, rows = recv_ref.shape[1:3]
    half = LANES // 2
    shape = (LANES, LANES)
    place = lanes_of(shape) % half
    row = rows_of(shape)
    valid = ((row < half) & (place < row)) | ((row >= half) & (place >= row - half))
    low = lanes_of((LANES, LANES)) < half
    low_half = lanes_of((rows, LANES)) < half

    def receiver(r, carry):
        total = jnp.zeros((4 * rows, LANES), jnp.float32)
        for k in range(PER_RECV):
            base = jnp.broadcast_to(taps_ref[r, k : k + 1, :], shape)
            band = pltpu.roll(base, half, 1, stride=1, stride_axis=0)
            band = jnp.where(valid, band, 0.0).astype(jnp.bfloat16)
            total = total + jnp.dot(
                fq_ref[slots[r, k]], band, preferred_element_type=jnp.float32
            )
        turned = half_turn(total[2 * rows :])
        both = total[: 2 * rows] + jnp.where(low, -turned, turned)
        first, second = both[:rows], both[rows:]
        re = jnp.where(low_half, first, half_turn(second))
        im = jnp.where(low_half, half_turn(first), second)
        out_ref[0, r] = (recv_ref[0, r].astype(jnp.float32) - re).astype(jnp.bfloat16)
        out_ref[1, r] = (recv_ref[1, r].astype(jnp.float32) - im).astype(jnp.bfloat16)
        return carry

    several(recv_count, 4, receiver)


def times_i(block):
    pieces = []
    for start in range(0, block.shape[1], LANES):
        turned = half_turn(block[:, start : start + LANES])
        pieces.append(jnp.where(lanes_of(turned.shape) < LANES // 2, -turned, turned))
    return jnp.concatenate(pieces, axis=1)


def complex_dot(left, right):
    return jnp.dot(left, right, precision=HIGHEST, preferred_element_type=jnp.float32)


def as_real(block):
    return jnp.concatenate([block, times_i(block)], axis=0)


def three_parts(value):
    parts = []
    for _ in range(3):
        part = value.astype(jnp.bfloat16).astype(jnp.float32)
        parts.append(part)
        value = value - part
    return parts


def panel_product(left, rows, place, start):
    panel = rows.shape[0]
    for shift in (panel, 2 * panel, 4 * panel):
        left = left + pltpu.roll(left, shift, 1)
    high, middle, low = three_parts(left)
    left = jnp.where(place < 3, high, jnp.where(place < 5, middle, low))
    left = jnp.where(place < 6, left, 0.0).astype(jnp.bfloat16)
    gap = jnp.zeros_like(rows)
    pieces = []
    for block in (rows, times_i(rows)):
        p, q, r = three_parts(block)
        pieces += [p, q, r, p, q, p, gap, gap]
    turn = start // panel
    pieces = pieces[len(pieces) - turn :] + pieces[: len(pieces) - turn]
    right = jnp.concatenate(pieces, axis=0).astype(jnp.bfloat16)
    return jnp.dot(left, right, preferred_element_type=jnp.float32)


def invert(blocks):
    size = blocks[0].shape[0]
    panel = 8
    shape = (panel, LANES)
    lane, row_id = lanes_of(shape), rows_of(shape)
    group = lanes_of(blocks[0].shape) % size // panel
    blocks = list(blocks)
    for start in range(0, size, panel):
        panels = [a[start : start + panel] for a in blocks]
        for t in range(0, panel, 2):
            j = start + t
            pair = (lane % size == j) | (lane % size == j + 1)
            for s, rows in enumerate(panels):
                re0, re1, im0, im1 = (
                    jnp.broadcast_to(rows[:, c : c + 1], shape)
                    for c in (j, j + 1, size + j, size + j + 1)
                )
                a, d = re0[t : t + 1], re1[t + 1 : t + 2]
                b_re, b_im = re1[t : t + 1], im1[t : t + 1]
                inverse = 1.0 / (a * d - (b_re * b_re + b_im * b_im))
                rest = jnp.where(pair, 0.0, rows)
                row0 = jnp.where(lane[:1] == j, 1.0, rest[t : t + 1])
                row1 = jnp.where(lane[:1] == j + 1, 1.0, rest[t + 1 : t + 2])
                row0_i, row1_i = times_i(row0), times_i(row1)
                new0 = (d * row0 - b_re * row1 - b_im * row1_i) * inverse
                new0_i = (d * row0_i - b_re * row1_i + b_im * row1) * inverse
                new1 = (a * row1 - b_re * row0 + b_im * row0_i) * inverse
                new1_i = (a * row1_i - b_re * row0_i - b_im * row0) * inverse
                rest = rest - (re0 * new0 + im0 * new0_i) - (re1 * new1 + im1 * new1_i)
                rest = jnp.where(row_id == t, new0, rest)
                panels[s] = jnp.where(row_id == t + 1, new1, rest)
        chosen = group == start // panel
        place = (lanes_of(blocks[0].shape) + (LANES - start)) % size // panel
        for s, (a, rows) in enumerate(zip(blocks, panels)):
            left = size - panel - start
            change = panel_product(jnp.where(chosen, a, 0.0), rows, place, start)
            rest = jnp.where(chosen, 0.0, a) - change
            above = [rest[:start]] if start > 0 else []
            below = [rest[start + panel :]] if left > 0 else []
            blocks[s] = jnp.concatenate(above + [rows] + below, axis=0)
    return blocks


def solve_kernel(slots, vr_ref, vi_ref, rhs_ref, out_ref, a_ref, d_ref):
    share = rhs_ref.shape[0]
    size = DELAYS
    window = math.isqrt(vr_ref.shape[0])
    shape = (size, LANES)
    lane, row_id = lanes_of(shape), rows_of(shape)
    low = lane < size
    unit = jnp.where(lane == row_id, jnp.float32(loading), 0.0)
    end = PER_RECV * LANES

    def build(index, carry):
        s, k = index // PER_RECV, index % PER_RECV
        start = pl.multiple_of(k * size, size)
        first = slots[s, k]
        for l in range(PER_RECV):
            at = first * window + slots[s, l]
            re = jnp.broadcast_to(vr_ref[at], shape)
            im = jnp.broadcast_to(vi_ref[at], shape)
            block = jnp.where(
                low,
                pltpu.roll(re, 0, 1, stride=1, stride_axis=0),
                pltpu.roll(im, size, 1, stride=1, stride_axis=0),
            )
            block = block + jnp.where(k == l, unit, 0.0)
            a_ref[s, pl.ds(start, size), l * LANES : (l + 1) * LANES] = block
        side = rhs_ref[s, pl.ds(start, size), :]
        a_ref[s, pl.ds(start, size), end : end + LANES] = jnp.where(
            lane == 0, side[:, 0:1], jnp.where(lane == size, side[:, 1:2], 0.0)
        )
        return carry

    lax.fori_loop(0, share * PER_RECV, build, 0)

    def eliminate(p, carry):
        at_row = pl.multiple_of(p * size, size)
        at_col = pl.multiple_of(p * LANES, LANES)
        blocks = [a_ref[s, pl.ds(at_row, size), pl.ds(at_col, LANES)] for s in range(share)]
        for s, block in enumerate(invert(blocks)):
            d_ref[s] = block
        for step in range(PER_RECV):

            @pl.when(p == step)
            def _():
                top, left = step * size, (step + 1) * LANES
                for s in range(share):
                    right = a_ref[s, top : top + size, left:]
                    scaled = complex_dot(d_ref[s], as_real(right))
                    a_ref[s, top : top + size, left:] = scaled
                    if step < PER_RECV - 1:
                        below = a_ref[s, top + size :, left - LANES : left]
                        a_ref[s, top + size :, left:] -= complex_dot(below, as_real(scaled))

        return carry

    lax.fori_loop(0, PER_RECV, eliminate, 0)
    for s in range(share):
        known = None
        for p in reversed(range(PER_RECV)):
            top, left = p * size, (p + 1) * LANES
            found = a_ref[s, top : top + size, end : end + LANES]
            if known is not None:
                found = found - complex_dot(a_ref[s, top : top + size, left:end], known)
            out_ref[s, top : top + size, :] = found
            found = as_real(found)
            known = found if known is None else jnp.concatenate([found, known], axis=0)


def kernel_call(body, outs, scalars, arrays, scratch=(), **params):
    spec_smem = pl.BlockSpec(memory_space=pltpu.SMEM)
    spec_vmem = pl.BlockSpec(memory_space=pltpu.VMEM)
    return pl.pallas_call(
        body,
        out_shape=outs,
        in_specs=[spec_smem] * len(scalars) + [spec_vmem] * len(arrays),
        out_specs=jax.tree.map(lambda _: spec_vmem, outs),
        scratch_shapes=list(scratch),
        compiler_params=pltpu.CompilerParams(vmem_limit_bytes=48 * MIB, **params),
    )(*scalars, *arrays)


def peer(offset):
    count = lax.axis_size("tm")
    return lax.rem(lax.axis_index("tm") + offset, count)


def greet():
    count = lax.axis_size("tm")
    barrier = pltpu.get_barrier_semaphore()
    for offset in range(1, count):
        pl.semaphore_signal(
            barrier,
            inc=1,
            device_id={"tm": peer(offset)},
            device_id_type=pl.DeviceIdType.MESH,
        )
    pl.semaphore_wait(barrier, count - 1)


def push(source, target, sends, arrivals, offset):
    copy = pltpu.make_async_remote_copy(
        src_ref=source,
        dst_ref=target,
        send_sem=sends.at[offset],
        recv_sem=arrivals.at[offset],
        device_id={"tm": peer(offset)},
        device_id_type=pl.DeviceIdType.MESH,
    )
    copy.start()
    return copy


def sum_kernel(
    corr_ref, cross_ref, corr_out, cross_out, corr_in, cross_in, s0, r0, s1, r1, s2, r2
):
    count, rows = corr_in.shape[:2]
    share = cross_in.shape[1]
    me = lax.axis_index("tm")
    own_rows = pl.ds(pl.multiple_of(me * rows, rows), rows)
    own_share = pl.ds(me * share, share)
    greet()
    copies = []
    for offset in range(1, count):
        to = peer(offset)
        their_rows = pl.ds(pl.multiple_of(to * rows, rows), rows)
        their_share = pl.ds(to * share, share)
        copies.append(push(corr_ref.at[their_rows], corr_in.at[offset], s0, r0, offset))
        copies.append(push(cross_ref.at[their_share], cross_in.at[offset], s1, r1, offset))
    for copy in copies[::2]:
        copy.wait()
    total = corr_ref[own_rows, :]
    for offset in range(1, count):
        total = total + corr_in[offset]
    corr_out[own_rows, :] = total
    spread = [
        push(corr_out.at[own_rows], corr_out.at[own_rows], s2, r2, offset)
        for offset in range(1, count)
    ]
    for copy in copies[1::2]:
        copy.wait()
    total = cross_ref[own_share]
    for offset in range(1, count):
        total = total + cross_in[offset]
    cross_out[...] = total
    for copy in spread:
        copy.wait()


def gather_kernel(in_ref, out_ref, sends, arrivals):
    count = out_ref.shape[0]
    me = lax.axis_index("tm")
    greet()
    copies = [push(in_ref, out_ref.at[me], sends, arrivals, o) for o in range(1, count)]
    out_ref[me] = in_ref[...]
    for copy in copies:
        copy.wait()


def window_sums(corr_part, cross_part):
    count = lax.axis_size("tm")
    shares = (cross_part.shape[0] // count,) + cross_part.shape[1:]
    flat = corr_part.reshape(-1, LANES)
    rows = flat.shape[0] // count
    corr, cross = kernel_call(
        sum_kernel,
        (
            jax.ShapeDtypeStruct(flat.shape, jnp.float32),
            jax.ShapeDtypeStruct(shares, jnp.float32),
        ),
        (),
        (flat, cross_part),
        (
            pltpu.VMEM((count, rows, LANES), jnp.float32),
            pltpu.VMEM((count,) + shares, jnp.float32),
        )
        + (pltpu.SemaphoreType.DMA((count,)),) * 6,
        collective_id=0,
        has_side_effects=True,
    )
    return corr.reshape(corr_part.shape), cross


def gathered_weights(solved):
    count = lax.axis_size("tm")
    return kernel_call(
        gather_kernel,
        jax.ShapeDtypeStruct((count,) + solved.shape, jnp.float32),
        (),
        (solved,),
        (pltpu.SemaphoreType.DMA((count,)),) * 2,
        collective_id=1,
        has_side_effects=True,
    )


def local(symbols, incidence, delays, gains, echoes):
    local_refs = remodulate(symbols)
    owned = local_refs.shape[0]
    length = local_refs.shape[2]
    rows = length // LANES
    taps_count = PER_RECV * DELAYS
    chan_count = lax.axis_size("chan")
    chan_index = lax.axis_index("chan")
    tm_count = lax.axis_size("tm")
    tm_index = lax.axis_index("tm")
    window_count = 2 * owned
    recv_count = echoes.shape[1]
    following = passed_along(local_refs, "chan", -1)
    window = jnp.concatenate([local_refs, following], axis=0)
    previous = from_behind(window[:, :, length - DELAYS :], "tm", 1)
    previous = jnp.pad(previous, ((0, 0), (0, 0), (LANES - DELAYS, 0)))[:, :, None, :]
    x = window.reshape(window_count, 2, rows, LANES)
    xp = jnp.concatenate([previous, x[:, :, :-1]], axis=2).astype(jnp.float32)
    x = x.astype(jnp.float32)
    owner_chan = incidence // owned
    slot = (owner_chan - chan_index) % chan_count * owned + incidence % owned
    received, corr_part, cross_part, frames = kernel_call(
        front_kernel,
        (
            jax.ShapeDtypeStruct((2, recv_count, rows, LANES), jnp.bfloat16),
            jax.ShapeDtypeStruct((window_count, window_count, LANES), jnp.float32),
            jax.ShapeDtypeStruct((recv_count, PER_RECV, LANES), jnp.float32),
            jax.ShapeDtypeStruct((window_count, 4 * rows, LANES), jnp.bfloat16),
        ),
        (slot, delays, gains),
        (x, xp, echoes.reshape(2, recv_count, rows, LANES)),
        (pltpu.VMEM((window_count, LANES, 4 * rows), jnp.bfloat16),),
    )
    share = recv_count // tm_count
    scale = 1.0 / (length * tm_count)
    corr, cross = window_sums(corr_part, cross_part)
    corr = corr * scale
    cross = cross * scale
    mine = lax.dynamic_slice_in_dim(slot, tm_index * share, share, 0)
    swapped = jnp.swapaxes(corr, 0, 1)
    gap = jnp.zeros(corr.shape[:2] + (1,), jnp.float32)

    def diagonals(ahead, behind, sign):
        line = jnp.concatenate(
            [ahead[..., :1], sign * behind[..., 1:], gap, jnp.flip(ahead[..., 1:], axis=-1)], axis=-1
        )
        return line.reshape(window_count * window_count, 1, LANES)

    vr = diagonals(swapped[..., :DELAYS], corr[..., :DELAYS], 1.0)
    vi = diagonals(swapped[..., DELAYS:], corr[..., DELAYS:], -1.0)
    rhs = cross.reshape(share, PER_RECV, 2, DELAYS).swapaxes(2, 3).reshape(share, taps_count, 2)
    solved = kernel_call(
        solve_kernel,
        jax.ShapeDtypeStruct((share, taps_count, LANES), jnp.float32),
        (mine,),
        (vr, vi, rhs),
        (
            pltpu.VMEM((share, taps_count, (PER_RECV + 1) * LANES), jnp.float32),
            pltpu.VMEM((share, DELAYS, LANES), jnp.float32),
        ),
    )
    local_weights = jnp.stack([solved[:, :, 0], solved[:, :, DELAYS]], axis=1)
    gathered = gathered_weights(local_weights.reshape(share * 2, taps_count))
    gathered = gathered.reshape(recv_count, 2, taps_count)
    weights = jnp.swapaxes(gathered, 0, 1)
    taps = gathered.astype(jnp.bfloat16).astype(jnp.float32)
    taps = taps.reshape(recv_count, 2, PER_RECV, DELAYS).swapaxes(1, 2)
    taps = taps.reshape(recv_count, PER_RECV, LANES)
    cancelled = kernel_call(
        back_kernel,
        jax.ShapeDtypeStruct((2, recv_count, rows, LANES), jnp.bfloat16),
        (slot,),
        (taps, frames, received),
    )
    return (cancelled.reshape(2, recv_count, length), weights)


def solution(mesh):
    in_specs = (
        P("chan", "tm"),
        P("chan", None),
        P("chan", None),
        P(None, "chan", None),
        P(None, "chan", "tm"),
    )
    out_specs = (P(None, "chan", "tm"), P(None, "chan", None))
    return jax.shard_map(local, mesh=mesh, in_specs=in_specs, out_specs=out_specs, check_vma=False)
```

```python
import math

import jax
import jax.numpy as jnp
from jax import lax
from jax.experimental import pallas as pl
from jax.experimental.pallas import tpu as pltpu
from jax.sharding import PartitionSpec as P

ACTIVE = 6817
DELAYS = 64
PER_RECV = 6


loading = 0.1
LANES = 128
MIB = 2**20
HIGHEST = lax.Precision.HIGHEST


def passed_along(array, axis, by):
    peers = lax.axis_size(axis)
    return lax.ppermute(array, axis, [(i, (i + by) % peers) for i in range(peers)])


def from_behind(block, axis, distance):
    devices = range(lax.axis_size(axis))
    route = [(i - distance, i) for i in devices if i - distance in devices]
    return lax.ppermute(block, axis, route)


def rotation_angle_grid(row_count, col_count, period):
    product = (
        jnp.arange(row_count, dtype=jnp.int32)[:, None]
        * jnp.arange(col_count, dtype=jnp.int32)[None, :]
    )
    phases = (product % period).astype(jnp.float32) * (2.0 * math.pi / period)
    return (jnp.cos(phases), jnp.sin(phases))


def complex_multiply_result(pattern, left_pair, right_pair):
    real_part = jnp.einsum(pattern, left_pair[0], right_pair[0], precision=HIGHEST) - jnp.einsum(
        pattern, left_pair[1], right_pair[1], precision=HIGHEST
    )
    imag_part = jnp.einsum(pattern, left_pair[0], right_pair[1], precision=HIGHEST) + jnp.einsum(
        pattern, left_pair[1], right_pair[0], precision=HIGHEST
    )
    return (real_part, imag_part)


def remodulate(symbols):
    emitter_number, length = symbols.shape
    column_entries = 128
    increment_spacing = length // column_entries
    inphase_amplitude = (2 * (symbols % 8) - 7).astype(jnp.float32) / math.sqrt(42.0)
    quadrature_amplitude = (2 * (symbols // 8) - 7).astype(jnp.float32) / math.sqrt(42.0)
    subcarrier = jnp.arange(length, dtype=jnp.int32) - length // 2
    occupied_tones = (jnp.abs(subcarrier) <= (ACTIVE - 1) // 2).astype(jnp.float32)
    tone_symbols = (
        (inphase_amplitude * occupied_tones).reshape(
            emitter_number, increment_spacing, column_entries
        ),
        (quadrature_amplitude * occupied_tones).reshape(
            emitter_number, increment_spacing, column_entries
        ),
    )
    partial_result = complex_multiply_result(
        "mb,nbd->nmd",
        rotation_angle_grid(increment_spacing, increment_spacing, increment_spacing),
        tone_symbols,
    )
    twiddle = rotation_angle_grid(increment_spacing, column_entries, length)
    partial_result = (
        partial_result[0] * twiddle[0] - partial_result[1] * twiddle[1],
        partial_result[0] * twiddle[1] + partial_result[1] * twiddle[0],
    )
    frequency_spectrum = complex_multiply_result(
        "pho,oj->phj",
        partial_result,
        rotation_angle_grid(column_entries, column_entries, column_entries),
    )
    alternate = (1 - 2 * (jnp.arange(length, dtype=jnp.int32) % 2)).astype(jnp.float32) / math.sqrt(
        ACTIVE
    )
    real_part = (
        jnp.swapaxes(frequency_spectrum[0], 1, 2).reshape(emitter_number, length) * alternate
    )
    imag_part = (
        jnp.swapaxes(frequency_spectrum[1], 1, 2).reshape(emitter_number, length) * alternate
    )
    return jnp.stack([real_part, imag_part], axis=1).astype(jnp.bfloat16)


def lanes_of(shape):
    return lax.broadcasted_iota(jnp.int32, shape, len(shape) - 1)


def rows_of(shape):
    return lax.broadcasted_iota(jnp.int32, shape, len(shape) - 2)


def half_turn(block):
    return pltpu.roll(block, LANES // 2, 1)


def several(count, together, body):
    together = math.gcd(count, together)

    def step(i, carry):
        for t in range(together):
            carry = body(i * together + t, carry)
        return carry

    lax.fori_loop(0, count // together, step, 0)


def signal_matrix(re, im):
    low = lanes_of(re.shape) < LANES // 2
    turned_re, turned_im = half_turn(re), half_turn(im)
    return jnp.concatenate(
        [
            jnp.where(low, re, turned_im),
            jnp.where(low, turned_re, im),
            jnp.where(low, im, -turned_re),
            jnp.where(low, turned_im, -re),
        ],
        axis=0,
    ).astype(jnp.bfloat16)


def fold_lags(product):
    half = LANES // 2
    shape = (half, LANES)
    earlier = lanes_of(shape) % half < rows_of(shape)
    total = jnp.where(earlier, half_turn(product[:half]), product[half:])
    rows = half // 2
    while rows >= 8:
        total = total[:rows] + pltpu.roll(total[rows:], LANES - rows, 1)
        rows //= 2
    for step in (4, 2, 1):
        total = total + pltpu.roll(pltpu.roll(total, LANES - step, 1), 8 - step, 0)
    return total[:1]


def front_kernel(
    slots, delays, gains, x_ref, xp_ref, echo_ref, recv_ref, corr_ref, cross_ref, fq_ref, ft_ref
):
    window, _, rows, _ = x_ref.shape
    recv_count = echo_ref.shape[1]
    lane = lanes_of((rows, LANES))
    low = lane < LANES // 2

    def frame(i, carry):
        parts = []
        for c in range(2):
            x = x_ref[i, c]
            parts += [half_turn(jnp.where(low, x, xp_ref[i, c])), x]
        whole = jnp.concatenate(parts, axis=0)
        fq_ref[i] = whole.astype(jnp.bfloat16)
        ft_ref[i] = whole.T.astype(jnp.bfloat16)
        return carry

    lax.fori_loop(0, window, frame, 0)

    def pairs(j, carry):
        matrix = signal_matrix(x_ref[j, 0], x_ref[j, 1])
        for i in range(window):
            product = jnp.dot(ft_ref[i], matrix, preferred_element_type=jnp.float32)
            corr_ref[j, i : i + 1, :] = fold_lags(product)
        return carry

    several(window, 2, pairs)

    def receiver(r, carry):
        re = jnp.zeros((rows, LANES), jnp.float32)
        im = jnp.zeros((rows, LANES), jnp.float32)
        for k in range(PER_RECV):
            s = slots[r, k]
            d = delays[r, k]
            g_re = gains[0, r, k]
            g_im = gains[1, r, k]
            wrapped = lane >= LANES - d
            y_re = pltpu.roll(jnp.where(wrapped, xp_ref[s, 0], x_ref[s, 0]), d, 1)
            y_im = pltpu.roll(jnp.where(wrapped, xp_ref[s, 1], x_ref[s, 1]), d, 1)
            re = re + (g_re * y_re - g_im * y_im)
            im = im + (g_re * y_im + g_im * y_re)
        re = (echo_ref[0, r].astype(jnp.float32) + re).astype(jnp.bfloat16)
        im = (echo_ref[1, r].astype(jnp.float32) + im).astype(jnp.bfloat16)
        recv_ref[0, r] = re
        recv_ref[1, r] = im
        matrix = signal_matrix(re.astype(jnp.float32), im.astype(jnp.float32))
        for k in range(PER_RECV):
            product = jnp.dot(ft_ref[slots[r, k]], matrix, preferred_element_type=jnp.float32)
            cross_ref[r, k : k + 1, :] = fold_lags(product)
        return carry

    several(recv_count, 2, receiver)


def back_kernel(slots, taps_ref, fq_ref, recv_ref, out_ref):
    recv_count, rows = recv_ref.shape[1:3]
    half = LANES // 2
    shape = (LANES, LANES)
    place = lanes_of(shape) % half
    row = rows_of(shape)
    valid = ((row < half) & (place < row)) | ((row >= half) & (place >= row - half))
    low = lanes_of((LANES, LANES)) < half
    low_half = lanes_of((rows, LANES)) < half

    def receiver(r, carry):
        total = jnp.zeros((4 * rows, LANES), jnp.float32)
        for k in range(PER_RECV):
            base = jnp.broadcast_to(taps_ref[r, k : k + 1, :], shape)
            band = pltpu.roll(base, half, 1, stride=1, stride_axis=0)
            band = jnp.where(valid, band, 0.0).astype(jnp.bfloat16)
            total = total + jnp.dot(
                fq_ref[slots[r, k]], band, preferred_element_type=jnp.float32
            )
        turned = half_turn(total[2 * rows :])
        both = total[: 2 * rows] + jnp.where(low, -turned, turned)
        first, second = both[:rows], both[rows:]
        re = jnp.where(low_half, first, half_turn(second))
        im = jnp.where(low_half, half_turn(first), second)
        out_ref[0, r] = (recv_ref[0, r].astype(jnp.float32) - re).astype(jnp.bfloat16)
        out_ref[1, r] = (recv_ref[1, r].astype(jnp.float32) - im).astype(jnp.bfloat16)
        return carry

    several(recv_count, 4, receiver)


def times_i(block):
    pieces = []
    for start in range(0, block.shape[1], LANES):
        turned = half_turn(block[:, start : start + LANES])
        pieces.append(jnp.where(lanes_of(turned.shape) < LANES // 2, -turned, turned))
    return jnp.concatenate(pieces, axis=1)


def complex_dot(left, right):
    return jnp.dot(left, right, precision=HIGHEST, preferred_element_type=jnp.float32)


def as_real(block):
    return jnp.concatenate([block, times_i(block)], axis=0)


def three_parts(value):
    parts = []
    for _ in range(3):
        part = value.astype(jnp.bfloat16).astype(jnp.float32)
        parts.append(part)
        value = value - part
    return parts


def panel_product(left, rows, place, start):
    panel = rows.shape[0]
    for shift in (panel, 2 * panel, 4 * panel):
        left = left + pltpu.roll(left, shift, 1)
    high, middle, low = three_parts(left)
    left = jnp.where(place < 3, high, jnp.where(place < 5, middle, low))
    left = jnp.where(place < 6, left, 0.0).astype(jnp.bfloat16)
    gap = jnp.zeros_like(rows)
    pieces = []
    for block in (rows, times_i(rows)):
        p, q, r = three_parts(block)
        pieces += [p, q, r, p, q, p, gap, gap]
    turn = start // panel
    pieces = pieces[len(pieces) - turn :] + pieces[: len(pieces) - turn]
    right = jnp.concatenate(pieces, axis=0).astype(jnp.bfloat16)
    return jnp.dot(left, right, preferred_element_type=jnp.float32)


def invert(blocks):
    size = blocks[0].shape[0]
    panel = 8
    shape = (panel, LANES)
    lane, row_id = lanes_of(shape), rows_of(shape)
    group = lanes_of(blocks[0].shape) % size // panel
    blocks = list(blocks)
    for start in range(0, size, panel):
        panels = [a[start : start + panel] for a in blocks]
        for t in range(0, panel, 2):
            j = start + t
            pair = (lane % size == j) | (lane % size == j + 1)
            for s, rows in enumerate(panels):
                re0, re1, im0, im1 = (
                    jnp.broadcast_to(rows[:, c : c + 1], shape)
                    for c in (j, j + 1, size + j, size + j + 1)
                )
                a, d = re0[t : t + 1], re1[t + 1 : t + 2]
                b_re, b_im = re1[t : t + 1], im1[t : t + 1]
                inverse = 1.0 / (a * d - (b_re * b_re + b_im * b_im))
                rest = jnp.where(pair, 0.0, rows)
                row0 = jnp.where(lane[:1] == j, 1.0, rest[t : t + 1])
                row1 = jnp.where(lane[:1] == j + 1, 1.0, rest[t + 1 : t + 2])
                row0_i, row1_i = times_i(row0), times_i(row1)
                new0 = (d * row0 - b_re * row1 - b_im * row1_i) * inverse
                new0_i = (d * row0_i - b_re * row1_i + b_im * row1) * inverse
                new1 = (a * row1 - b_re * row0 + b_im * row0_i) * inverse
                new1_i = (a * row1_i - b_re * row0_i - b_im * row0) * inverse
                rest = rest - (re0 * new0 + im0 * new0_i) - (re1 * new1 + im1 * new1_i)
                rest = jnp.where(row_id == t, new0, rest)
                panels[s] = jnp.where(row_id == t + 1, new1, rest)
        chosen = group == start // panel
        place = (lanes_of(blocks[0].shape) + (LANES - start)) % size // panel
        for s, (a, rows) in enumerate(zip(blocks, panels)):
            left = size - panel - start
            change = panel_product(jnp.where(chosen, a, 0.0), rows, place, start)
            rest = jnp.where(chosen, 0.0, a) - change
            above = [rest[:start]] if start > 0 else []
            below = [rest[start + panel :]] if left > 0 else []
            blocks[s] = jnp.concatenate(above + [rows] + below, axis=0)
    return blocks


def solve_kernel(slots, vr_ref, vi_ref, rhs_ref, out_ref, a_ref, d_ref):
    share = rhs_ref.shape[0]
    size = DELAYS
    window = math.isqrt(vr_ref.shape[0])
    shape = (size, LANES)
    lane, row_id = lanes_of(shape), rows_of(shape)
    low = lane < size
    unit = jnp.where(lane == row_id, jnp.float32(loading), 0.0)
    end = PER_RECV * LANES

    def build(index, carry):
        s, k = index // PER_RECV, index % PER_RECV
        start = pl.multiple_of(k * size, size)
        first = slots[s, k]
        for l in range(PER_RECV):
            at = first * window + slots[s, l]
            re = jnp.broadcast_to(vr_ref[at], shape)
            im = jnp.broadcast_to(vi_ref[at], shape)
            block = jnp.where(
                low,
                pltpu.roll(re, 0, 1, stride=1, stride_axis=0),
                pltpu.roll(im, size, 1, stride=1, stride_axis=0),
            )
            block = block + jnp.where(k == l, unit, 0.0)
            a_ref[s, pl.ds(start, size), l * LANES : (l + 1) * LANES] = block
        side = rhs_ref[s, pl.ds(start, size), :]
        a_ref[s, pl.ds(start, size), end : end + LANES] = jnp.where(
            lane == 0, side[:, 0:1], jnp.where(lane == size, side[:, 1:2], 0.0)
        )
        return carry

    lax.fori_loop(0, share * PER_RECV, build, 0)

    def eliminate(p, carry):
        at_row = pl.multiple_of(p * size, size)
        at_col = pl.multiple_of(p * LANES, LANES)
        blocks = [a_ref[s, pl.ds(at_row, size), pl.ds(at_col, LANES)] for s in range(share)]
        for s, block in enumerate(invert(blocks)):
            d_ref[s] = block
        for step in range(PER_RECV):

            @pl.when(p == step)
            def _():
                top, left = step * size, (step + 1) * LANES
                for s in range(share):
                    right = a_ref[s, top : top + size, left:]
                    scaled = complex_dot(d_ref[s], as_real(right))
                    a_ref[s, top : top + size, left:] = scaled
                    if step < PER_RECV - 1:
                        below = a_ref[s, top + size :, left - LANES : left]
                        a_ref[s, top + size :, left:] -= complex_dot(below, as_real(scaled))

        return carry

    lax.fori_loop(0, PER_RECV, eliminate, 0)
    for s in range(share):
        known = None
        for p in reversed(range(PER_RECV)):
            top, left = p * size, (p + 1) * LANES
            found = a_ref[s, top : top + size, end : end + LANES]
            if known is not None:
                found = found - complex_dot(a_ref[s, top : top + size, left:end], known)
            out_ref[s, top : top + size, :] = found
            found = as_real(found)
            known = found if known is None else jnp.concatenate([found, known], axis=0)


def kernel_call(body, outs, scalars, arrays, scratch=(), **params):
    spec_smem = pl.BlockSpec(memory_space=pltpu.SMEM)
    spec_vmem = pl.BlockSpec(memory_space=pltpu.VMEM)
    return pl.pallas_call(
        body,
        out_shape=outs,
        in_specs=[spec_smem] * len(scalars) + [spec_vmem] * len(arrays),
        out_specs=jax.tree.map(lambda _: spec_vmem, outs),
        scratch_shapes=list(scratch),
        compiler_params=pltpu.CompilerParams(vmem_limit_bytes=48 * MIB, **params),
    )(*scalars, *arrays)


def peer(offset):
    count = lax.axis_size("tm")
    return lax.rem(lax.axis_index("tm") + offset, count)


def greet():
    count = lax.axis_size("tm")
    barrier = pltpu.get_barrier_semaphore()
    for offset in range(1, count):
        pl.semaphore_signal(
            barrier,
            inc=1,
            device_id={"tm": peer(offset)},
            device_id_type=pl.DeviceIdType.MESH,
        )
    pl.semaphore_wait(barrier, count - 1)


def push(source, target, sends, arrivals, offset):
    copy = pltpu.make_async_remote_copy(
        src_ref=source,
        dst_ref=target,
        send_sem=sends.at[offset],
        recv_sem=arrivals.at[offset],
        device_id={"tm": peer(offset)},
        device_id_type=pl.DeviceIdType.MESH,
    )
    copy.start()
    return copy


def sum_kernel(
    corr_ref, cross_ref, corr_out, cross_out, corr_in, cross_in, s0, r0, s1, r1, s2, r2
):
    count, rows = corr_in.shape[:2]
    share = cross_in.shape[1]
    me = lax.axis_index("tm")
    own_rows = pl.ds(pl.multiple_of(me * rows, rows), rows)
    own_share = pl.ds(me * share, share)
    greet()
    copies = []
    for offset in range(1, count):
        to = peer(offset)
        their_rows = pl.ds(pl.multiple_of(to * rows, rows), rows)
        their_share = pl.ds(to * share, share)
        copies.append(push(corr_ref.at[their_rows], corr_in.at[offset], s0, r0, offset))
        copies.append(push(cross_ref.at[their_share], cross_in.at[offset], s1, r1, offset))
    for copy in copies[::2]:
        copy.wait()
    total = corr_ref[own_rows, :]
    for offset in range(1, count):
        total = total + corr_in[offset]
    corr_out[own_rows, :] = total
    spread = [
        push(corr_out.at[own_rows], corr_out.at[own_rows], s2, r2, offset)
        for offset in range(1, count)
    ]
    for copy in copies[1::2]:
        copy.wait()
    total = cross_ref[own_share]
    for offset in range(1, count):
        total = total + cross_in[offset]
    cross_out[...] = total
    for copy in spread:
        copy.wait()


def gather_kernel(in_ref, out_ref, sends, arrivals):
    count = out_ref.shape[0]
    me = lax.axis_index("tm")
    greet()
    copies = [push(in_ref, out_ref.at[me], sends, arrivals, o) for o in range(1, count)]
    out_ref[me] = in_ref[...]
    for copy in copies:
        copy.wait()


def window_sums(corr_part, cross_part):
    count = lax.axis_size("tm")
    shares = (cross_part.shape[0] // count,) + cross_part.shape[1:]
    flat = corr_part.reshape(-1, LANES)
    rows = flat.shape[0] // count
    corr, cross = kernel_call(
        sum_kernel,
        (
            jax.ShapeDtypeStruct(flat.shape, jnp.float32),
            jax.ShapeDtypeStruct(shares, jnp.float32),
        ),
        (),
        (flat, cross_part),
        (
            pltpu.VMEM((count, rows, LANES), jnp.float32),
            pltpu.VMEM((count,) + shares, jnp.float32),
        )
        + (pltpu.SemaphoreType.DMA((count,)),) * 6,
        collective_id=0,
        has_side_effects=True,
    )
    return corr.reshape(corr_part.shape), cross


def gathered_weights(solved):
    count = lax.axis_size("tm")
    return kernel_call(
        gather_kernel,
        jax.ShapeDtypeStruct((count,) + solved.shape, jnp.float32),
        (),
        (solved,),
        (pltpu.SemaphoreType.DMA((count,)),) * 2,
        collective_id=1,
        has_side_effects=True,
    )


def local(symbols, incidence, delays, gains, echoes):
    local_refs = remodulate(symbols)
    owned = local_refs.shape[0]
    length = local_refs.shape[2]
    rows = length // LANES
    taps_count = PER_RECV * DELAYS
    chan_count = lax.axis_size("chan")
    chan_index = lax.axis_index("chan")
    tm_count = lax.axis_size("tm")
    tm_index = lax.axis_index("tm")
    window_count = 2 * owned
    recv_count = echoes.shape[1]
    following = passed_along(local_refs, "chan", -1)
    window = jnp.concatenate([local_refs, following], axis=0)
    previous = from_behind(window[:, :, length - DELAYS :], "tm", 1)
    previous = jnp.pad(previous, ((0, 0), (0, 0), (LANES - DELAYS, 0)))[:, :, None, :]
    x = window.reshape(window_count, 2, rows, LANES)
    xp = jnp.concatenate([previous, x[:, :, :-1]], axis=2).astype(jnp.float32)
    x = x.astype(jnp.float32)
    owner_chan = incidence // owned
    slot = (owner_chan - chan_index) % chan_count * owned + incidence % owned
    received, corr_part, cross_part, frames = kernel_call(
        front_kernel,
        (
            jax.ShapeDtypeStruct((2, recv_count, rows, LANES), jnp.bfloat16),
            jax.ShapeDtypeStruct((window_count, window_count, LANES), jnp.float32),
            jax.ShapeDtypeStruct((recv_count, PER_RECV, LANES), jnp.float32),
            jax.ShapeDtypeStruct((window_count, 4 * rows, LANES), jnp.bfloat16),
        ),
        (slot, delays, gains),
        (x, xp, echoes.reshape(2, recv_count, rows, LANES)),
        (pltpu.VMEM((window_count, LANES, 4 * rows), jnp.bfloat16),),
    )
    share = recv_count // tm_count
    scale = 1.0 / (length * tm_count)
    corr, cross = window_sums(corr_part, cross_part)
    corr = corr * scale
    cross = cross * scale
    mine = lax.dynamic_slice_in_dim(slot, tm_index * share, share, 0)
    swapped = jnp.swapaxes(corr, 0, 1)
    gap = jnp.zeros(corr.shape[:2] + (1,), jnp.float32)

    def diagonals(ahead, behind, sign):
        line = jnp.concatenate(
            [ahead[..., :1], sign * behind[..., 1:], gap, jnp.flip(ahead[..., 1:], axis=-1)], axis=-1
        )
        return line.reshape(window_count * window_count, 1, LANES)

    vr = diagonals(swapped[..., :DELAYS], corr[..., :DELAYS], 1.0)
    vi = diagonals(swapped[..., DELAYS:], corr[..., DELAYS:], -1.0)
    rhs = cross.reshape(share, PER_RECV, 2, DELAYS).swapaxes(2, 3).reshape(share, taps_count, 2)
    solved = kernel_call(
        solve_kernel,
        jax.ShapeDtypeStruct((share, taps_count, LANES), jnp.float32),
        (mine,),
        (vr, vi, rhs),
        (
            pltpu.VMEM((share, taps_count, (PER_RECV + 1) * LANES), jnp.float32),
            pltpu.VMEM((share, DELAYS, LANES), jnp.float32),
        ),
    )
    local_weights = jnp.stack([solved[:, :, 0], solved[:, :, DELAYS]], axis=1)
    gathered = gathered_weights(local_weights.reshape(share * 2, taps_count))
    gathered = gathered.reshape(recv_count, 2, taps_count)
    weights = jnp.swapaxes(gathered, 0, 1)
    taps = gathered.astype(jnp.bfloat16).astype(jnp.float32)
    taps = taps.reshape(recv_count, 2, PER_RECV, DELAYS).swapaxes(1, 2)
    taps = taps.reshape(recv_count, PER_RECV, LANES)
    cancelled = kernel_call(
        back_kernel,
        jax.ShapeDtypeStruct((2, recv_count, rows, LANES), jnp.bfloat16),
        (slot,),
        (taps, frames, received),
    )
    return (cancelled.reshape(2, recv_count, length), weights)


def solution(mesh):
    in_specs = (
        P("chan", "tm"),
        P("chan", None),
        P("chan", None),
        P(None, "chan", None),
        P(None, "chan", "tm"),
    )
    out_specs = (P(None, "chan", "tm"), P(None, "chan", None))
    return jax.shard_map(local, mesh=mesh, in_specs=in_specs, out_specs=out_specs, check_vma=False)
```
